32 devices in a mesh: context: 4 (over z), seq: 4 (over y, x), tensor: 2 (over core).
Axes of the slice: x: 2, y: 2, z: 4, core: 2. Of those that a mesh axis runs over, the one named last changes fastest.
Arguments:
- queries: bfloat16 [4096, 2048], P(('seq', 'context'), 'tensor'), parts along dimension 0, may hold values from -9 to 9
- key_states: bfloat16 [4096, 512], P(('seq', 'context'), 'tensor'), parts along dimension 0, may hold values from -4 to 4
- value_states: bfloat16 [4096, 512], P(('seq', 'context'), 'tensor'), parts along dimension 0, may hold values from -6 to 6
- segment_ids: int32 [4096], P('seq'), parts along dimension 0, may hold values from 0 to 3, never falling along the last dimension, each value on 1 to 768 neighbouring positions
- hidden: bfloat16 [4096, 2048], P(('seq', 'context')), parts along dimension 0, may hold values from -6 to 6
- attn_out_weight: bfloat16 [2048, 2048], P('tensor'), may hold values from -0.125 to 0.125
- norm_gain: bfloat16 [2048], replicated, may hold values from 0.5 to 1.5
- gate_weight: bfloat16 [2048, 4096], P(None, 'tensor'), may hold values from -0.125 to 0.125
- inner_weight: bfloat16 [2048, 4096], P(None, 'tensor'), may hold values from -0.125 to 0.125
- state_proj_weight: bfloat16 [2048, 256], replicated, may hold values from -0.125 to 0.125
- step_weight: bfloat16 [2048, 64], P(None, 'tensor'), may hold values from -0.125 to 0.125
- conv_inner: bfloat16 [4, 4096], P(None, 'tensor'), may hold values from -3 to 3
- conv_state: bfloat16 [4, 256], replicated, may hold values from -3 to 3
- step_bias: float32 [64], P('tensor'), may hold values from -4 to 0
- decay_log: float32 [64], P('tensor'), may hold values from -12 to 3
- skip_gain: float32 [64], P('tensor'), may hold values from 0.5 to 1.5
- out_gain: bfloat16 [4096], P('tensor'), may hold values from 0.5 to 1.5
Outputs:
- residual: bfloat16 [4096, 2048], P(('seq', 'context')), parts along dimension 0
- mixed: bfloat16 [4096, 4096], P(('seq', 'context'), 'tensor'), parts along dimension 0
The draws below stay inside these ranges and needn't reach their ends.
There are 4 independent parts, one for each index of `seq`. The reference program is written for one: setup_inputs(seed, part) draws one part's arguments, and reference() takes and returns one part's arrays. A program takes and returns all parts, laid end to end along the dimension named above; an argument that names none is the same for every part. Nothing has to cross between parts.
Inputs may be any that keep to these rules, and one draw needn't show every extreme that they name: `segment_ids`: segment ids never fall along a sequence.
All inputs are finite; a program needn't handle non-finite values.
Results may differ from the reference program's by a relative error of at most 0.012.
Values may be sent and summed in bfloat16 or wider, within the bound.
A program may use at most 128 MiB of HBM per device.

```python
import math
import jax
import jax.numpy as jnp
import numpy as np
from jax import lax

D = 2048
ATT_HEADS = 16
KV_HEADS = 4
HEAD_DIM = 128
SSM_HEADS = 64
SSM_HEAD_DIM = 64
STATE = 128
CONV = 4
WINDOW = 2048
SEGMENTS = 4
TOK_DEV = 256
LENGTH = 1024
D_INNER = 4096


def draw_queries(key, part):
    shape = (LENGTH, ATT_HEADS * HEAD_DIM)
    base = jnp.clip(jax.random.normal(jax.random.fold_in(key, 1), shape, jnp.float32), -4.0, 4.0)
    return base.astype(jnp.bfloat16)


def draw_key_states(key, part):
    shape = (LENGTH, KV_HEADS * HEAD_DIM)
    base = jnp.clip(jax.random.normal(jax.random.fold_in(key, 2), shape, jnp.float32), -4.0, 4.0)
    return base.astype(jnp.bfloat16)


def draw_step_bias(key, part):
    return jax.random.uniform(jax.random.fold_in(key, 3), (SSM_HEADS,), jnp.float32, -4.0, 0.0)


def draw_decay_log(key, part):
    reach = jax.random.uniform(jax.random.fold_in(key, 4), (SSM_HEADS,), jnp.float32, math.log(0.3), math.log(300.0))
    return reach - math.log(LENGTH)


def levels(key, extent, split, least, largest):
    def one(position, blocks):
        draws = jax.random.uniform(jax.random.fold_in(jax.random.fold_in(key, 6), position), (blocks,), jnp.float32, least / len(split), largest / len(split))
        return jnp.repeat(jnp.exp(draws), extent[position] // blocks).reshape((-1,) + (1,) * (len(extent) - position - 1))

    level = one(*split[0])
    for cut in split[1:]:
        level = level * one(*cut)
    return level


def profile(number_of, total, bound, lean):
    loads = [(1 << 20) // math.isqrt(grade ** lean) + 1 for grade in range(2, number_of + 1)]
    surplus, given = total - bound - (number_of - 1), [1] * (number_of - 1)
    while surplus > 0:
        candidates = [i for i in range(number_of - 1) if given[i] < bound]
        whole, remaining = sum([loads[i] for i in candidates]), surplus
        for i in candidates:
            extra = min(bound - given[i], max(1, remaining * loads[i] // whole), surplus)
            given[i] = given[i] + extra
            surplus = surplus - extra
    return np.array([bound] + given)


def uneven(stream_key, amount, total, most, skew):
    if amount == 2:
        one = jax.random.randint(stream_key, (), max(1, total - most), min(most, total - 1) + 1)
        return jnp.stack([one, total - one])
    sizes = jnp.asarray(profile(amount, total, most, skew), jnp.int32)
    twos = (amount - 1) // 2
    source_of, taker = sizes[1:1 + 2 * twos:2], sizes[2:2 + 2 * twos:2]
    margin = jnp.minimum(source_of - 1, most - taker)
    moved = jax.random.randint(jax.random.fold_in(stream_key, 1), (twos,), 0, 1 << 20) % (margin + 1)
    sizes = sizes.at[1:1 + 2 * twos:2].set(source_of - moved).at[2:2 + 2 * twos:2].set(taker + moved)
    return sizes[jax.random.permutation(jax.random.fold_in(stream_key, 2), amount)]


def centred(rng, shape, width, bound, cuts=(), held_as=jnp.bfloat16):
    values = width * jax.random.normal(rng, shape, jnp.float32)
    if cuts:
        values = values * levels(rng, shape, cuts, -0.22, 0.18)
    return jnp.clip(values, -bound, bound).astype(held_as)


def setup_inputs(seed: int = 0, part: int = 0) -> dict:
    key_list = jax.random.split(jax.random.key(seed), 18)
    own_keys = jax.random.split(jax.random.fold_in(key_list[17], part), 18)
    queries = draw_queries(jax.random.fold_in(jax.random.fold_in(key_list[17], part), 71), part)
    key_states = draw_key_states(jax.random.fold_in(jax.random.fold_in(key_list[17], part), 71), part)
    value_states = centred(own_keys[2], (LENGTH, KV_HEADS * HEAD_DIM), 1.0, 6.0, ((0, 4), (1, 2)))
    segment_ids = jnp.searchsorted(jnp.cumsum(uneven(own_keys[3], SEGMENTS, LENGTH, 3 * LENGTH // 4, 0)), jnp.arange(LENGTH), side="right").astype(jnp.int32)
    hidden = centred(own_keys[4], (LENGTH, D), 1.0, 6.0, ((0, 4),))
    attn_out_weight = centred(key_list[5], (ATT_HEADS * HEAD_DIM, D), (ATT_HEADS * HEAD_DIM) ** -0.5, 0.125, ((0, 2),))
    norm_gain = jnp.clip(1.0 + 0.1 * jax.random.normal(key_list[6], (D,), jnp.float32), 0.5, 1.5).astype(jnp.bfloat16)
    gate_weight = centred(key_list[7], (D, D_INNER), D ** -0.5, 0.125, ((1, 2),))
    inner_weight = centred(key_list[8], (D, D_INNER), D ** -0.5, 0.125, ((1, 2),))
    state_proj_weight = centred(key_list[9], (D, 2 * STATE), D ** -0.5, 0.125)
    step_weight = centred(key_list[10], (D, SSM_HEADS), D ** -0.5, 0.125, ((1, 2),))
    conv_inner = centred(key_list[11], (CONV, D_INNER), CONV ** -0.5, 3.0, ((1, 2),))
    conv_state = centred(key_list[12], (CONV, 2 * STATE), CONV ** -0.5, 3.0)
    step_bias = draw_step_bias(jax.random.fold_in(key_list[17], 71), part)
    decay_log = draw_decay_log(jax.random.fold_in(key_list[17], 71), part)
    skip_gain = jnp.clip(0.5 + 1.0 * jax.random.uniform(key_list[15], (SSM_HEADS,), jnp.float32) ** levels(key_list[15], (SSM_HEADS,), ((0, 2),), -0.2, 0.2), 0.5, 1.5)
    out_gain = jnp.clip(1.0 + 0.1 * jax.random.normal(key_list[16], (D_INNER,), jnp.float32), 0.5, 1.5).astype(jnp.bfloat16)
    return dict(queries=queries, key_states=key_states, value_states=value_states, segment_ids=segment_ids, hidden=hidden, attn_out_weight=attn_out_weight, norm_gain=norm_gain, gate_weight=gate_weight, inner_weight=inner_weight, state_proj_weight=state_proj_weight, step_weight=step_weight, conv_inner=conv_inner, conv_state=conv_state, step_bias=step_bias, decay_log=decay_log, skip_gain=skip_gain, out_gain=out_gain)


EPSILON = 1e-05

def attend(query_rows, key_rows, value_rows, query_pos, key_pos, query_seg, key_seg):
    groups = ATT_HEADS // KV_HEADS
    count = query_rows.shape[0]
    local_heads = key_rows.shape[1] // HEAD_DIM
    shaped_q = query_rows.reshape(count, local_heads, groups, HEAD_DIM).astype(jnp.float32)
    shaped_k = key_rows.reshape(-1, local_heads, HEAD_DIM).astype(jnp.float32)
    shaped_v = value_rows.reshape(-1, local_heads, HEAD_DIM).astype(jnp.float32)
    scores = jnp.einsum('tgjd,sgd->gjts', shaped_q, shaped_k) * HEAD_DIM ** (-0.5)
    allowed = (key_pos[None, :] <= query_pos[:, None]) & (query_pos[:, None] - key_pos[None, :] < WINDOW)
    allowed = allowed & (key_seg[None, :] == query_seg[:, None])
    scores = jnp.where(allowed, scores, -jnp.inf)
    highest = lax.optimization_barrier(jnp.max(scores, axis=-1, keepdims=True))
    weights = jnp.exp(scores - highest)
    probs = (weights / lax.optimization_barrier(jnp.sum(weights, axis=-1, keepdims=True))).astype(jnp.bfloat16)
    blended = jnp.einsum('gjts,sgd->tgjd', probs.astype(jnp.float32), shaped_v)
    return blended.astype(jnp.bfloat16).reshape(count, -1)

def causal_conv(raw_rows, taps, seg_rows):
    count = raw_rows.shape[0] - CONV + 1
    target = seg_rows[CONV - 1:]
    total = jnp.zeros((count, raw_rows.shape[1]), jnp.float32)
    for tap in range(CONV):
        keep = (seg_rows[tap:tap + count] == target).astype(jnp.float32)
        total = total + taps[tap].astype(jnp.float32)[None, :] * raw_rows[tap:tap + count].astype(jnp.float32) * keep[:, None]
    return jax.nn.silu(total).astype(jnp.bfloat16)

def local_terms(shaped, read_in, read_out, step, rate, seg_rows):
    count = shaped.shape[0]
    running = jnp.cumsum(rate, axis=0)
    order = jnp.arange(count, dtype=jnp.int32)
    same = (seg_rows[:, None] == seg_rows[None, :]) & (order[:, None] >= order[None, :])
    gap = running.T[:, :, None] - running.T[:, None, :]
    decay = jnp.where(same[None], jnp.exp(jnp.where(same[None], gap, 0.0)), 0.0)
    pairwise = jnp.einsum('tn,sn->ts', read_out.astype(jnp.float32), read_in.astype(jnp.float32))
    mixing = (decay * pairwise[None] * step.T[:, None, :]).astype(jnp.bfloat16)
    within = jnp.einsum('hts,shp->thp', mixing.astype(jnp.float32), shaped.astype(jnp.float32))
    tail = jnp.exp(running[-1][None, :] - running) * (seg_rows == seg_rows[-1]).astype(jnp.float32)[:, None]
    weighted = ((tail * step)[:, :, None] * shaped.astype(jnp.float32)).astype(jnp.bfloat16)
    end_state = jnp.einsum('thp,tn->hpn', weighted.astype(jnp.float32), read_in.astype(jnp.float32))
    return (within, running, end_state)

def reference(queries, key_states, value_states, segment_ids, hidden, attn_out_weight, norm_gain, gate_weight, inner_weight, state_proj_weight, step_weight, conv_inner, conv_state, step_bias, decay_log, skip_gain, out_gain):
    length = hidden.shape[0]
    block = TOK_DEV
    blocks = length // block
    filler = jnp.zeros((WINDOW, key_states.shape[1]), key_states.dtype)
    padded_keys = jnp.concatenate([filler, key_states])
    padded_values = jnp.concatenate([filler, value_states])
    padded_seg = jnp.concatenate([jnp.full((WINDOW,), -1, jnp.int32), segment_ids])

    def one_block(index):
        start = (index * block).astype(jnp.int32)
        query_rows = lax.dynamic_slice_in_dim(queries, start, block, 0)
        key_rows = lax.dynamic_slice_in_dim(padded_keys, start, WINDOW + block, 0)
        value_rows = lax.dynamic_slice_in_dim(padded_values, start, WINDOW + block, 0)
        query_seg = lax.dynamic_slice_in_dim(segment_ids, start, block, 0)
        key_seg = lax.dynamic_slice_in_dim(padded_seg, start, WINDOW + block, 0)
        query_pos = start + jnp.arange(block, dtype=jnp.int32)
        key_pos = start - WINDOW + jnp.arange(WINDOW + block, dtype=jnp.int32)
        return attend(query_rows, key_rows, value_rows, query_pos, key_pos, query_seg, key_seg)
    attended = lax.map(one_block, jnp.arange(blocks, dtype=jnp.int32)).reshape(length, -1)
    projected = jnp.dot(attended, attn_out_weight, preferred_element_type=jnp.float32)
    residual = (hidden.astype(jnp.float32) + projected).astype(jnp.bfloat16)
    wide = residual.astype(jnp.float32)
    normed = (wide * lax.rsqrt(lax.optimization_barrier(jnp.mean(wide * wide, axis=-1, keepdims=True)) + EPSILON) * norm_gain.astype(jnp.float32)[None, :]).astype(jnp.bfloat16)
    gate = jnp.dot(normed, gate_weight, preferred_element_type=jnp.float32).astype(jnp.bfloat16)
    inner_raw = jnp.dot(normed, inner_weight, preferred_element_type=jnp.float32).astype(jnp.bfloat16)
    state_raw = jnp.dot(normed, state_proj_weight, preferred_element_type=jnp.float32).astype(jnp.bfloat16)
    step_raw = jnp.dot(normed, step_weight, preferred_element_type=jnp.float32)
    step = jax.nn.softplus(step_raw + step_bias[None, :])
    rate = -jnp.exp(decay_log)[None, :] * step
    conv_seg = jnp.concatenate([jnp.full((CONV - 1,), -1, jnp.int32), segment_ids])
    inner = causal_conv(jnp.concatenate([jnp.zeros((CONV - 1, inner_raw.shape[1]), jnp.bfloat16), inner_raw]), conv_inner, conv_seg)
    state_conv = causal_conv(jnp.concatenate([jnp.zeros((CONV - 1, state_raw.shape[1]), jnp.bfloat16), state_raw]), conv_state, conv_seg)
    read_in = state_conv[:, :STATE]
    read_out = state_conv[:, STATE:]
    shaped = inner.reshape(length, SSM_HEADS, SSM_HEAD_DIM)

    def ssd_block(carry, pieces):
        state, prior_seg = carry
        block_inner, block_in, block_out, block_step, block_rate, block_seg = pieces
        within, running, end_state = local_terms(block_inner, block_in, block_out, block_step, block_rate, block_seg)
        entry = jnp.exp(running) * (block_seg == prior_seg).astype(jnp.float32)[:, None]
        state_low = lax.optimization_barrier(state.astype(jnp.bfloat16)).astype(jnp.float32)
        incoming = jnp.einsum('tn,hpn->thp', block_out.astype(jnp.float32), state_low) * entry[:, :, None]
        end_decay = jnp.exp(running[-1]) * (block_seg[-1] == prior_seg).astype(jnp.float32)
        new_state = end_decay[:, None, None] * state + end_state
        return ((new_state, block_seg[-1]), within + incoming)
    pieces = (shaped.reshape(blocks, block, SSM_HEADS, SSM_HEAD_DIM), read_in.reshape(blocks, block, STATE), read_out.reshape(blocks, block, STATE), step.reshape(blocks, block, SSM_HEADS), rate.reshape(blocks, block, SSM_HEADS), segment_ids.reshape(blocks, block))
    start_state = jnp.zeros((SSM_HEADS, SSM_HEAD_DIM, STATE), jnp.float32)
    _, outputs = lax.scan(ssd_block, (start_state, jnp.int32(-1)), pieces)
    ssm_out = outputs.reshape(length, SSM_HEADS, SSM_HEAD_DIM) + skip_gain[None, :, None] * shaped.astype(jnp.float32)
    gated = ssm_out.reshape(length, -1) * jax.nn.silu(gate.astype(jnp.float32))
    squares = lax.optimization_barrier(jnp.sum(gated * gated, axis=-1))
    mixed = (gated * lax.rsqrt(squares / D_INNER + EPSILON)[:, None] * out_gain.astype(jnp.float32)[None, :]).astype(jnp.bfloat16)
    return (residual, mixed)
```

```python
import functools

import jax
import jax.numpy as jnp
from jax import lax
from jax.experimental import pallas as pl
from jax.experimental.pallas import tpu as pltpu
from jax.sharding import PartitionSpec as P

ATT_HEADS = 16
KV_HEADS = 4
HEAD_DIM = 128
STATE = 128
CONV = 4
WINDOW = 2048
EPSILON = 1e-05
LANES = 128
HALO = 16
PAD = 8
LOW = -1e30
F32 = jnp.float32
BF16 = jnp.bfloat16


def dot(a, b):
    return jnp.dot(a, b, preferred_element_type=F32)


def silu(x):
    return x / (1.0 + jnp.exp(-x))


def wide(x, width):
    return jnp.concatenate([x] * (width // LANES), axis=1)


def split(x, parts):
    out = []
    for _ in range(parts):
        piece = x.astype(BF16)
        out.append(piece)
        x = x - piece.astype(F32)
    return out


def body(
    cfg,
    q_hbm, k_hbm, v_hbm, seg_ref, hid_hbm, wo_hbm, gain_ref, wg_hbm, wi_hbm, ws_hbm, wt_ref,
    ci_ref, cs_ref, bias_ref, decay_ref, skip_ref, og_ref,
    res_hbm, mix_hbm,
    q, kbuf, vbuf, hid, wo, wg, wi, ws, att, m_s, l_s, acc, mask, res, normed,
    raw, sraw, halo_out, halo_in, segc, keep, step, run, runT, stepT, gate, inner, rin, rinT, rout,
    pm, state, carry_in, carry_out, within, gated, sq, sq_in,
    local_sem, ksend, krecv, vsend, vrecv, wsend, wrecv, asend, arecv, hsend, hrecv,
    csend, crecv, ssend, srecv,
):
    C, TP, reach = cfg["context"], cfg["tensor"], cfg["reach"]
    T, D = hid.shape
    DI = wi.shape[1]
    SH = wt_ref.shape[1]
    PH = DI // SH
    heads = q.shape[1] // HEAD_DIM
    groups = ATT_HEADS // KV_HEADS
    NC, _, W = carry_in.shape
    i = lax.axis_index("context")
    core = lax.axis_index("tensor")
    has_next = i + 1 < C
    has_prev = i > 0
    partners = [lax.rem(core + k, TP) for k in range(1, TP)]

    def remote(src, dst, s, r, **where):
        return pltpu.make_async_remote_copy(
            src_ref=src, dst_ref=dst, send_sem=s, recv_sem=r,
            device_id=where, device_id_type=pl.DeviceIdType.MESH,
        )

    barrier = pltpu.get_barrier_semaphore()

    def greet(**where):
        pl.semaphore_signal(
            barrier, inc=1, device_id=where, device_id_type=pl.DeviceIdType.MESH
        )

    @pl.when(has_next)
    def _():
        greet(context=i + 1)

    @pl.when(has_prev)
    def _():
        greet(context=i - 1)

    for partner in partners:
        greet(tensor=partner)

    locals_ = [
        pltpu.make_async_copy(src, dst, local_sem.at[n])
        for n, (src, dst) in enumerate(
            [(q_hbm, q), (k_hbm, kbuf.at[0]), (v_hbm, vbuf.at[0]), (wo_hbm, wo.at[core]),
             (hid_hbm, hid), (ws_hbm, ws), (wi_hbm, wi), (wg_hbm, wg)]
        )
    ]
    for copy in locals_[:3]:
        copy.start()

    pl.semaphore_wait(
        barrier, has_next.astype(jnp.int32) + has_prev.astype(jnp.int32) + TP - 1
    )

    def hop(d):
        to = i + 1
        return (
            remote(kbuf.at[d], kbuf.at[d + 1], ksend.at[d], krecv.at[d], context=to),
            remote(vbuf.at[d], vbuf.at[d + 1], vsend.at[d], vrecv.at[d], context=to),
        )

    locals_[1].wait()
    locals_[2].wait()
    if reach > 0:
        @pl.when(has_next)
        def _():
            for copy in hop(0):
                copy.start()

    for copy in locals_[3:]:
        copy.start()
    wcopies = [
        remote(wo_hbm, wo.at[core], wsend.at[n], wrecv.at[n], tensor=partner)
        for n, partner in enumerate(partners)
    ]
    for copy in wcopies:
        copy.start()

    rows = lax.broadcasted_iota(jnp.int32, (T, T), 0)
    cols = lax.broadcasted_iota(jnp.int32, (T, T), 1)

    def seg_row(block):
        return seg_ref[:, pl.ds(pl.multiple_of(block * T, LANES), T)].astype(F32)

    def column(row):
        return jnp.sum(jnp.where(rows == cols, row, 0.0), axis=1, keepdims=True)

    own_row = seg_row(i)
    own_col = column(own_row)
    prev_col = jnp.where(has_prev, column(seg_row(jnp.maximum(i - 1, 0))), -1.0)
    segc[PAD:, :] = jnp.broadcast_to(own_col, (T, LANES))
    segc[:PAD, :] = jnp.broadcast_to(prev_col[T - PAD :, :], (PAD, LANES))
    for tap in range(CONV):
        keep[tap] = (segc[pl.ds(PAD - CONV + 1 + tap, T), :] == segc[PAD:, :]).astype(F32)

    m_s[...] = jnp.full(m_s.shape, LOW, F32)
    l_s[...] = jnp.zeros(l_s.shape, F32)
    acc[...] = jnp.zeros(acc.shape, F32)
    scale = HEAD_DIM ** (-0.5)

    def attend(d):
        gap = d * T + rows - cols
        key_row = seg_row(i - d)
        allowed = (gap >= 0) & (gap < WINDOW) & (segc[PAD:, :1] == key_row)
        mask[...] = jnp.where(allowed, 0.0, LOW)

        def one(h, carry):
            at = pl.multiple_of(h * HEAD_DIM, HEAD_DIM)
            kat = pl.multiple_of((h // groups) * HEAD_DIM, HEAD_DIM)
            s = lax.dot_general(
                q[:, pl.ds(at, HEAD_DIM)], kbuf[d, :, pl.ds(kat, HEAD_DIM)],
                (((1,), (1,)), ((), ())), preferred_element_type=F32,
            )
            s = s * scale + mask[...]
            old = m_s[h]
            new = jnp.maximum(old, jnp.max(s, axis=1, keepdims=True))
            alpha = jnp.exp(old - new)
            p = jnp.exp(s - wide(new, T))
            m_s[h] = new
            l_s[h] = l_s[h] * alpha + jnp.sum(p, axis=1, keepdims=True)
            acc[h] = acc[h] * alpha + dot(p.astype(BF16), vbuf[d, :, pl.ds(kat, HEAD_DIM)])
            return carry

        lax.fori_loop(0, heads, one, 0, unroll=2)

    locals_[0].wait()
    attend(0)

    if reach > 0:
        def arrive(d, carry):
            @pl.when(i >= d)
            def _():
                for copy in hop(d - 1):
                    copy.wait_recv()

                @pl.when(has_next & (d < reach))
                def _():
                    for copy in hop(d):
                        copy.start()

                attend(d)

            return carry

        lax.fori_loop(1, reach + 1, arrive, 0)

    def finish(h, carry):
        at = pl.multiple_of(h * HEAD_DIM, HEAD_DIM)
        att[core, :, pl.ds(at, HEAD_DIM)] = (acc[h] / l_s[h]).astype(BF16)
        return carry

    lax.fori_loop(0, heads, finish, 0, unroll=2)
    acopies = [
        remote(att.at[core], att.at[core], asend.at[n], arecv.at[n], tensor=partner)
        for n, partner in enumerate(partners)
    ]
    for copy in acopies:
        copy.start()
    locals_[3].wait()
    locals_[4].wait()
    for copy in wcopies:
        copy.wait()
    for copy in acopies:
        copy.wait()

    def project(c, squares):
        at = pl.ds(pl.multiple_of(c * W, LANES), W)
        total = dot(att[0], wo[0, :, at])
        for k in range(1, TP):
            total = total + dot(att[k], wo[k, :, at])
        r = (hid[:, at].astype(F32) + total).astype(BF16)
        res[:, at] = r
        r = r.astype(F32)
        return squares + jnp.sum(r * r, axis=1, keepdims=True)

    squares = lax.fori_loop(0, D // W, project, jnp.zeros((T, 1), F32))
    res_copy = pltpu.make_async_copy(res, res_hbm, local_sem.at[8])
    res_copy.start()
    inv = lax.rsqrt(squares / D + EPSILON)

    def norm(c, carry):
        at = pl.ds(pl.multiple_of(c * W, LANES), W)
        normed[:, at] = (res[:, at].astype(F32) * inv * gain_ref[:, at].astype(F32)).astype(BF16)
        return carry

    lax.fori_loop(0, D // W, norm, 0)

    locals_[5].wait()
    x = dot(normed[...], ws[...]).astype(BF16)
    sraw[PAD:, :] = x.astype(F32)
    halo_out[:, DI:] = x[T - HALO :, :]
    locals_[6].wait()

    def project_inner(c, carry):
        at = pl.ds(pl.multiple_of(c * W, LANES), W)
        y = dot(normed[...], wi[:, at]).astype(BF16)
        raw[PAD:, at] = y.astype(F32)
        halo_out[:, at] = y[T - HALO :, :]
        return carry

    lax.fori_loop(0, NC, project_inner, 0)
    halo = remote(halo_out, halo_in, hsend.at[0], hrecv.at[0], context=i + 1)

    @pl.when(has_next)
    def _():
        halo.start()

    raw_step = dot(normed[...], wt_ref[...]) + bias_ref[...]
    soft = jnp.maximum(raw_step, 0.0) + jnp.log1p(jnp.exp(-jnp.abs(raw_step)))
    step[...] = jnp.zeros(step.shape, F32)
    step[:, :SH] = soft
    run[...] = jnp.zeros(run.shape, F32)
    run[:, :SH] = -jnp.exp(decay_ref[...]) * soft
    causal = rows >= cols
    tri = jnp.where(causal, 1.0, 0.0).astype(BF16)
    running = sum(dot(tri, piece) for piece in split(run[...], 3))
    run[...] = running
    runT[...] = running.T
    stepT[...] = step[...].T

    locals_[7].wait()

    def project_gate(c, carry):
        at = pl.ds(pl.multiple_of(c * W, LANES), W)
        gate[:, at] = dot(normed[...], wg[:, at]).astype(BF16)
        return carry

    lax.fori_loop(0, NC, project_gate, 0)

    @pl.when(has_prev)
    def _():
        halo.wait_recv()
        raw[:PAD, :] = halo_in[:, :DI].astype(F32)[HALO - PAD :, :]
        sraw[:PAD, :] = halo_in[:, DI:].astype(F32)[HALO - PAD :, :]

    @pl.when(jnp.logical_not(has_prev))
    def _():
        raw[:PAD, :] = jnp.zeros((PAD, DI), F32)
        sraw[:PAD, :] = jnp.zeros((PAD, sraw.shape[1]), F32)

    def conv(ref, taps, at, width):
        total = jnp.zeros((T, width), F32)
        for tap in range(CONV):
            total = total + (
                taps[tap : tap + 1, at].astype(F32)
                * ref[pl.ds(PAD - CONV + 1 + tap, T), at]
                * wide(keep[tap], width)
            )
        return silu(total)

    sc = conv(sraw, cs_ref, pl.ds(0, 2 * STATE), 2 * STATE)
    rin[...] = sc[:, :STATE].astype(BF16)
    rinT[...] = sc[:, :STATE].T.astype(BF16)
    rout[...] = sc[:, STATE:].astype(BF16)
    pairwise = lax.dot_general(
        rout[...], rin[...], (((1,), (1,)), ((), ())), preferred_element_type=F32
    )
    pm[...] = jnp.where(causal & (segc[PAD:, :1] == own_row), pairwise, 0.0)

    last = run[T - 1 : T, :]
    prior = segc[PAD - 1 : PAD, :]
    tail = jnp.exp(last - run[...]) * step[...]
    tail = jnp.where(segc[PAD:, :] == segc[PAD + T - 1 : PAD + T, :], tail, 0.0)
    tail = split(tail, 2)
    entry = split(jnp.where(segc[PAD:, :] == prior, jnp.exp(run[...]), 0.0), 2)
    end = jnp.where(segc[PAD + T - 1 : PAD + T, :] == prior, jnp.exp(last), 0.0)
    end = split(jnp.broadcast_to(end, (HALO, LANES)), 3)
    gain = jnp.concatenate([skip_ref[...], jnp.zeros((1, LANES - SH), F32)], axis=1)
    gain = split(jnp.broadcast_to(gain, (HALO, LANES)), 3)
    head_row = lax.broadcasted_iota(jnp.int32, (LANES, W), 0) * PH
    head_col = lax.broadcasted_iota(jnp.int32, (LANES, W), 1)

    def expand(pieces, c):
        offset = head_col + c * W - head_row
        pick = jnp.where((offset >= 0) & (offset < PH), 1.0, 0.0).astype(BF16)
        return sum(dot(piece, pick) for piece in pieces)

    def convolve(c, carry):
        at = pl.ds(pl.multiple_of(c * W, LANES), W)
        value = conv(raw, ci_ref, at, W).astype(BF16)
        inner[:, at] = value
        weighted = (expand(tail, c) * value.astype(F32)).astype(BF16)
        state[c] = dot(rinT[...], weighted)
        return carry

    lax.fori_loop(0, NC, convolve, 0)

    def onward(c):
        return remote(carry_out.at[c], carry_in.at[c], csend.at[c], crecv.at[c], context=i + 1)

    @pl.when(jnp.logical_not(has_prev))
    def _():
        carry_in[...] = jnp.zeros(carry_in.shape, BF16)

        @pl.when(has_next)
        def _():
            for c in range(NC):
                carry_out[c] = state[c].astype(BF16)
                onward(c).start()

    lane = lax.broadcasted_iota(jnp.int32, (T, LANES), 1)
    per = LANES // PH

    def mixing(h):
        col = jnp.sum(jnp.where(lane == h, run[...], 0.0), axis=1, keepdims=True)
        decay = jnp.exp(jnp.minimum(col - runT[pl.ds(h, 1), :], 0.0))
        return (decay * pm[...] * stepT[pl.ds(h, 1), :]).astype(BF16)

    def pair(n, carry):
        at = pl.ds(pl.multiple_of(n * LANES, LANES), LANES)
        value = inner[:, at]
        total = dot(mixing(n * per), value)
        for k in range(1, per):
            total = jnp.where(lane >= k * PH, dot(mixing(n * per + k), value), total)
        within[:, at] = total
        return carry

    def chunk(c, squares):
        lax.fori_loop(c * (W // LANES), (c + 1) * (W // LANES), pair, 0)
        at = pl.ds(pl.multiple_of(c * W, LANES), W)

        @pl.when(has_prev)
        def _():
            onward(c).wait_recv()

            @pl.when(has_next)
            def _():
                moved = expand(end, c)[:1, :] * carry_in[c].astype(F32) + state[c]
                carry_out[c] = moved.astype(BF16)
                onward(c).start()

        y = within[:, at] + dot(rout[...], carry_in[c]) * expand(entry, c)
        y = y + expand(gain, c)[:1, :] * inner[:, at].astype(F32)
        y = y * silu(gate[:, at].astype(F32))
        gated[:, at] = y
        return squares + jnp.sum(y * y, axis=1, keepdims=True)

    total = lax.fori_loop(0, NC, chunk, jnp.zeros((T, 1), F32))
    sq[...] = jnp.broadcast_to(total, (T, LANES))
    scopies = [
        remote(sq, sq_in.at[n], ssend.at[n], srecv.at[n], tensor=partner)
        for n, partner in enumerate(partners)
    ]
    for copy in scopies:
        copy.start()
    for copy in scopies:
        copy.wait()
    grand = sq[...]
    for n in range(TP - 1):
        grand = grand + sq_in[n]
    factor = wide(lax.rsqrt(grand / (DI * TP) + EPSILON), W)

    def scale_out(c, carry):
        at = pl.ds(pl.multiple_of(c * W, LANES), W)
        inner[:, at] = (gated[:, at] * factor * og_ref[:, at].astype(F32)).astype(BF16)
        return carry

    lax.fori_loop(0, NC, scale_out, 0)
    mix_copy = pltpu.make_async_copy(inner, mix_hbm, local_sem.at[9])
    mix_copy.start()

    @pl.when(has_next)
    def _():
        halo.wait_send()
        for c in range(NC):
            onward(c).wait_send()
        for d in range(reach):
            @pl.when(i >= d)
            def _():
                for copy in hop(d):
                    copy.wait_send()

    res_copy.wait()
    mix_copy.wait()


def per_device(cfg, *args):
    (queries, key_states, value_states, segment_ids, hidden, attn_out_weight, norm_gain,
     gate_weight, inner_weight, state_proj_weight, step_weight, conv_inner, conv_state,
     step_bias, decay_log, skip_gain, out_gain) = args
    T, D = hidden.shape
    DI = inner_weight.shape[1]
    SN = state_proj_weight.shape[1]
    KW = key_states.shape[1]
    TP, C = cfg["tensor"], cfg["context"]
    reach = min(-(-(WINDOW - 1) // T), C - 1)
    cfg = dict(cfg, reach=reach)
    heads = queries.shape[1] // HEAD_DIM
    W = min(512, DI, D)
    NC = DI // W
    hbm = pl.BlockSpec(memory_space=pl.ANY)
    vmem = pl.BlockSpec(memory_space=pltpu.VMEM)
    hops = max(reach, 1)
    peers = max(TP - 1, 1)
    V = pltpu.VMEM
    dma = pltpu.SemaphoreType.DMA
    scratch = [
        V(queries.shape, BF16), V((reach + 1, T, KW), BF16), V((reach + 1, T, KW), BF16),
        V((T, D), BF16), V((TP,) + attn_out_weight.shape, BF16), V(gate_weight.shape, BF16),
        V(inner_weight.shape, BF16), V(state_proj_weight.shape, BF16),
        V((TP,) + queries.shape, BF16),
        V((heads, T, LANES), F32), V((heads, T, LANES), F32), V((heads, T, HEAD_DIM), F32),
        V((T, T), F32), V((T, D), BF16), V((T, D), BF16),
        V((PAD + T, DI), F32), V((PAD + T, SN), F32), V((HALO, DI + SN), BF16),
        V((HALO, DI + SN), BF16), V((PAD + T, LANES), F32), V((CONV, T, LANES), F32),
        V((T, LANES), F32), V((T, LANES), F32), V((LANES, T), F32), V((LANES, T), F32),
        V((T, DI), BF16), V((T, DI), BF16), V((T, STATE), BF16), V((STATE, T), BF16),
        V((T, STATE), BF16), V((T, T), F32), V((NC, STATE, W), F32), V((NC, STATE, W), BF16),
        V((NC, STATE, W), BF16), V((T, DI), F32), V((T, DI), F32), V((T, LANES), F32),
        V((peers, T, LANES), F32),
        dma((10,)), dma((hops,)), dma((hops,)), dma((hops,)), dma((hops,)),
        dma((peers,)), dma((peers,)), dma((peers,)), dma((peers,)), dma((1,)), dma((1,)),
        dma((NC,)), dma((NC,)), dma((peers,)), dma((peers,)),
    ]
    row = lambda x: x.reshape(1, -1)
    return pl.pallas_call(
        functools.partial(body, cfg),
        out_shape=(
            jax.ShapeDtypeStruct((T, D), BF16),
            jax.ShapeDtypeStruct((T, DI), BF16),
        ),
        in_specs=[hbm, hbm, hbm, vmem, hbm, hbm, vmem, hbm, hbm, hbm] + [vmem] * 7,
        out_specs=(hbm, hbm),
        scratch_shapes=scratch,
        compiler_params=pltpu.CompilerParams(
            collective_id=0, has_side_effects=True, vmem_limit_bytes=60 * 1024 * 1024
        ),
    )(
        queries, key_states, value_states, row(segment_ids), hidden, attn_out_weight,
        row(norm_gain), gate_weight, inner_weight, state_proj_weight, step_weight,
        conv_inner, conv_state, row(step_bias), row(decay_log), row(skip_gain), row(out_gain),
    )


def solution(mesh):
    cfg = {"context": mesh.shape["context"], "tensor": mesh.shape["tensor"]}
    both, tensor = P(("seq", "context"), "tensor"), P("tensor")
    in_specs = (
        both, both, both, P("seq"), P(("seq", "context"), None), P("tensor", None), P(),
        P(None, "tensor"), P(None, "tensor"), P(), P(None, "tensor"), P(None, "tensor"), P(),
        tensor, tensor, tensor, tensor,
    )
    return jax.shard_map(
        functools.partial(per_device, cfg), mesh=mesh, in_specs=in_specs,
        out_specs=(P(("seq", "context"), None), both), check_vma=False,
    )
```

```python
import functools

import jax
import jax.numpy as jnp
from jax import lax
from jax.experimental import pallas as pl
from jax.experimental.pallas import tpu as pltpu
from jax.sharding import PartitionSpec as P

ATT_HEADS = 16
KV_HEADS = 4
HEAD_DIM = 128
STATE = 128
CONV = 4
WINDOW = 2048
EPSILON = 1e-05
LANES = 128
HALO = 16
PAD = 8
PIECES = 4
LOW = -1e30
F32 = jnp.float32
BF16 = jnp.bfloat16


def dot(a, b):
    return jnp.dot(a, b, preferred_element_type=F32)


def silu(x):
    half = 0.5 * x
    return half + half * jnp.tanh(half)


def wide(x, width):
    return jnp.concatenate([x] * (width // LANES), axis=1)


def split(x, parts):
    out = []
    for _ in range(parts):
        piece = x.astype(BF16)
        out.append(piece)
        x = x - piece.astype(F32)
    return out


def body(
    cfg,
    q_hbm, k_hbm, v_hbm, seg_ref, hid_hbm, wo_hbm, gain_ref, wg_hbm, wi_hbm, ws_hbm, wt_ref,
    ci_ref, cs_ref, bias_ref, decay_ref, skip_ref, og_ref,
    res_hbm, mix_hbm,
    q, kbuf, vbuf, hid, wo, wg, wi, ws, att, m_s, l_s, acc, mask, res, normed,
    raw, sraw, halo_out, halo_in, segc, keep, step, run, runT, stepT, inner, rin, rinT, rout,
    pm, state, carry_in, carry_out, within, gated, sq, sq_in, part, pick, coef, gains, og, skip,
    local_sem, ksend, krecv, vsend, vrecv, wsend, wrecv, asend, arecv, hsend, hrecv,
    csend, crecv, ssend, srecv,
):
    C, TP, reach = cfg["context"], cfg["tensor"], cfg["reach"]
    T, D = hid.shape
    DI = wi.shape[1]
    SH = wt_ref.shape[0]
    PH = DI // SH
    heads = q.shape[1] // HEAD_DIM
    groups = ATT_HEADS // KV_HEADS
    NC, _, W = carry_in.shape
    i = lax.axis_index("context")
    core = lax.axis_index("tensor")
    has_next = i + 1 < C
    has_prev = i > 0
    partners = [lax.rem(core + k, TP) for k in range(1, TP)]

    def remote(src, dst, s, r, **where):
        return pltpu.make_async_remote_copy(
            src_ref=src, dst_ref=dst, send_sem=s, recv_sem=r,
            device_id=where, device_id_type=pl.DeviceIdType.MESH,
        )

    barrier = pltpu.get_barrier_semaphore()

    def greet(**where):
        pl.semaphore_signal(
            barrier, inc=1, device_id=where, device_id_type=pl.DeviceIdType.MESH
        )

    @pl.when(has_next)
    def _():
        greet(context=i + 1)

    @pl.when(has_prev)
    def _():
        greet(context=i - 1)

    for partner in partners:
        greet(tensor=partner)

    locals_ = [
        pltpu.make_async_copy(src, dst, local_sem.at[n])
        for n, (src, dst) in enumerate(
            [(q_hbm, q), (k_hbm, kbuf.at[0]), (v_hbm, vbuf.at[0]), (wo_hbm, wo.at[core]),
             (hid_hbm, hid), (ws_hbm, ws), (wi_hbm, wi), (wg_hbm, wg)]
        )
    ]
    for copy in locals_[:3]:
        copy.start()

    pl.semaphore_wait(
        barrier, has_next.astype(jnp.int32) + has_prev.astype(jnp.int32) + TP - 1
    )

    def hop(d):
        to = i + 1
        return (
            remote(kbuf.at[d], kbuf.at[d + 1], ksend.at[d], krecv.at[d], context=to),
            remote(vbuf.at[d], vbuf.at[d + 1], vsend.at[d], vrecv.at[d], context=to),
        )

    locals_[1].wait()
    locals_[2].wait()
    if reach > 0:
        @pl.when(has_next)
        def _():
            for copy in hop(0):
                copy.start()

    for copy in locals_[3:]:
        copy.start()
    wcopies = [
        remote(wo_hbm, wo.at[core], wsend.at[n], wrecv.at[n], tensor=partner)
        for n, partner in enumerate(partners)
    ]
    for copy in wcopies:
        copy.start()

    rows = lax.broadcasted_iota(jnp.int32, (T, T), 0)
    cols = lax.broadcasted_iota(jnp.int32, (T, T), 1)

    def seg_row(block):
        return seg_ref[:, pl.ds(pl.multiple_of(block * T, LANES), T)].astype(F32)

    def column(row):
        return jnp.sum(jnp.where(rows == cols, row, 0.0), axis=1, keepdims=True)

    own_row = seg_row(i)
    own_col = column(own_row)
    prev_col = jnp.where(has_prev, column(seg_row(jnp.maximum(i - 1, 0))), -1.0)
    segc[PAD:, :] = jnp.broadcast_to(own_col, (T, LANES))
    segc[:PAD, :] = jnp.broadcast_to(prev_col[T - PAD :, :], (PAD, LANES))
    for tap in range(CONV - 1):
        keep[tap] = (segc[pl.ds(PAD - CONV + 1 + tap, T), :] == segc[PAD:, :]).astype(F32)

    gains[...] = gain_ref[...].astype(F32)
    og[...] = og_ref[...].astype(F32)

    def row_of(ref, c):
        per = W // LANES
        return jnp.concatenate([ref[pl.ds(c * per + k, 1), :] for k in range(per)], axis=1)

    head_row = lax.broadcasted_iota(jnp.int32, (LANES, W), 0) * PH
    head_col = lax.broadcasted_iota(jnp.int32, (LANES, W), 1)

    def make_pick(c, carry):
        offset = head_col + c * W - head_row
        chosen = jnp.where((offset >= 0) & (offset < PH), 1.0, 0.0).astype(BF16)
        pick[c, :LANES, :] = chosen
        pick[c, LANES:, :] = chosen
        return carry

    lax.fori_loop(0, NC, make_pick, 0)

    def pieces(x):
        return jnp.concatenate(split(x, 2), axis=1)

    gain = jnp.concatenate([skip_ref[...], jnp.zeros((1, LANES - SH), F32)], axis=1)
    gain = pieces(jnp.broadcast_to(gain, (HALO, LANES)))
    for c in range(NC):
        skip[c] = dot(gain, pick[c])

    m_s[...] = jnp.full(m_s.shape, LOW, F32)
    l_s[...] = jnp.zeros(l_s.shape, F32)
    acc[...] = jnp.zeros(acc.shape, F32)
    scale = HEAD_DIM ** (-0.5)

    def attend(d):
        gap = d * T + rows - cols
        key_row = seg_row(i - d)
        allowed = (gap >= 0) & (gap < WINDOW) & (segc[PAD:, :1] == key_row)
        mask[...] = jnp.where(allowed, 0.0, LOW)

        def one(h, carry):
            at = pl.multiple_of(h * HEAD_DIM, HEAD_DIM)
            kat = pl.multiple_of((h // groups) * HEAD_DIM, HEAD_DIM)
            s = lax.dot_general(
                q[:, pl.ds(at, HEAD_DIM)], kbuf[d, :, pl.ds(kat, HEAD_DIM)],
                (((1,), (1,)), ((), ())), preferred_element_type=F32,
            )
            s = s * scale + mask[...]
            old = m_s[h]
            new = jnp.maximum(old, jnp.max(s, axis=1, keepdims=True))
            alpha = jnp.exp(old - new)
            p = jnp.exp(s - wide(new, T))
            m_s[h] = new
            l_s[h] = l_s[h] * alpha + jnp.sum(p, axis=1, keepdims=True)
            acc[h] = acc[h] * alpha + dot(p.astype(BF16), vbuf[d, :, pl.ds(kat, HEAD_DIM)])
            return carry

        lax.fori_loop(0, heads, one, 0, unroll=4)

    locals_[0].wait()
    attend(0)

    if reach > 0:
        def arrive(d, carry):
            @pl.when(i >= d)
            def _():
                for copy in hop(d - 1):
                    copy.wait_recv()

                @pl.when(has_next & (d < reach))
                def _():
                    for copy in hop(d):
                        copy.start()

                attend(d)

            return carry

        lax.fori_loop(1, reach + 1, arrive, 0)

    def finish(h, carry):
        at = pl.multiple_of(h * HEAD_DIM, HEAD_DIM)
        att[core, :, pl.ds(at, HEAD_DIM)] = (acc[h] / l_s[h]).astype(BF16)
        return carry

    lax.fori_loop(0, heads, finish, 0, unroll=2)
    acopies = [
        remote(att.at[core], att.at[core], asend.at[n], arecv.at[n], tensor=partner)
        for n, partner in enumerate(partners)
    ]
    for copy in acopies:
        copy.start()
    locals_[3].wait()

    def project_own(c, carry):
        at = pl.ds(pl.multiple_of(c * W, LANES), W)
        part[:, at] = dot(att[core], wo[core, :, at])
        return carry

    lax.fori_loop(0, D // W, project_own, 0)
    locals_[4].wait()
    for copy in wcopies:
        copy.wait()
    for copy in acopies:
        copy.wait()

    def project(c, squares):
        at = pl.ds(pl.multiple_of(c * W, LANES), W)
        total = part[:, at]
        for partner in partners:
            total = total + dot(att[partner], wo[partner, :, at])
        r = (hid[:, at].astype(F32) + total).astype(BF16)
        res[:, at] = r
        r = r.astype(F32)
        return squares + jnp.sum(r * r, axis=1, keepdims=True)

    squares = lax.fori_loop(0, D // W, project, jnp.zeros((T, 1), F32))
    res_copy = pltpu.make_async_copy(res, res_hbm, local_sem.at[8])
    res_copy.start()
    inv = lax.rsqrt(squares / D + EPSILON)

    def norm(c, carry):
        at = pl.ds(pl.multiple_of(c * W, LANES), W)
        normed[:, at] = (res[:, at].astype(F32) * inv * row_of(gains, c)).astype(BF16)
        return carry

    lax.fori_loop(0, D // W, norm, 0)

    locals_[5].wait()
    x = dot(normed[...], ws[...]).astype(BF16)
    sraw[PAD:, :] = x.astype(F32)
    halo_out[:, DI:] = x[T - HALO :, :]
    locals_[6].wait()

    def project_inner(c, carry):
        at = pl.ds(pl.multiple_of(c * W, LANES), W)
        y = dot(normed[...], wi[:, at]).astype(BF16)
        raw[PAD:, at] = y.astype(F32)
        halo_out[:, at] = y[T - HALO :, :]
        return carry

    lax.fori_loop(0, NC, project_inner, 0)
    halo = remote(halo_out, halo_in, hsend.at[0], hrecv.at[0], context=i + 1)

    @pl.when(has_next)
    def _():
        halo.start()

    raw_step = lax.dot_general(
        normed[...], wt_ref[...], (((1,), (1,)), ((), ())), preferred_element_type=F32
    ) + bias_ref[...]
    soft = jnp.maximum(raw_step, 0.0) + jnp.log1p(jnp.exp(-jnp.abs(raw_step)))
    step[...] = jnp.zeros(step.shape, F32)
    step[:, :SH] = soft
    run[...] = jnp.zeros(run.shape, F32)
    run[:, :SH] = -jnp.exp(decay_ref[...]) * soft
    causal = rows >= cols
    tri = jnp.where(causal, 1.0, 0.0).astype(BF16)
    running = sum(dot(tri, piece) for piece in split(run[...], 3))
    run[...] = running
    runT[...] = running.T
    stepT[...] = step[...].T

    locals_[7].wait()

    def project_gate(c, carry):
        at = pl.ds(pl.multiple_of(c * W, LANES), W)
        gated[:, at] = silu(dot(normed[...], wg[:, at]).astype(BF16).astype(F32))
        return carry

    lax.fori_loop(0, NC, project_gate, 0)

    @pl.when(has_prev)
    def _():
        halo.wait_recv()
        raw[:PAD, :] = halo_in[:, :DI].astype(F32)[HALO - PAD :, :]
        sraw[:PAD, :] = halo_in[:, DI:].astype(F32)[HALO - PAD :, :]

    @pl.when(jnp.logical_not(has_prev))
    def _():
        raw[:PAD, :] = jnp.zeros((PAD, DI), F32)
        sraw[:PAD, :] = jnp.zeros((PAD, sraw.shape[1]), F32)

    def conv(ref, taps, at, width):
        total = taps[CONV - 1 : CONV, at].astype(F32) * ref[PAD:, at]
        for tap in range(CONV - 1):
            total = total + (
                taps[tap : tap + 1, at].astype(F32)
                * ref[pl.ds(PAD - CONV + 1 + tap, T), at]
                * wide(keep[tap], width)
            )
        return silu(total)

    sc = conv(sraw, cs_ref, pl.ds(0, 2 * STATE), 2 * STATE)
    rin[...] = sc[:, :STATE].astype(BF16)
    rinT[...] = sc[:, :STATE].T.astype(BF16)
    rout[...] = sc[:, STATE:].astype(BF16)
    pairwise = lax.dot_general(
        rout[...], rin[...], (((1,), (1,)), ((), ())), preferred_element_type=F32
    )
    pm[...] = jnp.where(causal & (segc[PAD:, :1] == own_row), pairwise, 0.0)

    last = run[T - 1 : T, :]
    prior = segc[PAD - 1 : PAD, :]
    tail = jnp.exp(last - run[...]) * step[...]
    tail = jnp.where(segc[PAD:, :] == segc[PAD + T - 1 : PAD + T, :], tail, 0.0)
    B = T // 2
    middle = run[B - 1 : B, :]
    coef[:T, :] = pieces(tail)
    coef[T : 2 * T, :] = pieces(jnp.where(segc[PAD:, :] == prior, jnp.exp(run[...]), 0.0))
    coef[2 * T : 2 * T + B, :] = pieces(jnp.exp(middle - run[:B, :]) * step[:B, :])
    coef[2 * T + B :, :] = pieces(jnp.exp(run[B:, :] - middle))
    end = jnp.where(segc[PAD + T - 1 : PAD + T, :] == prior, jnp.exp(last), 0.0)
    end = pieces(jnp.broadcast_to(end, (HALO, LANES)))
    cross = pm[B:, :B].astype(BF16)

    def convolve(c, carry):
        at = pl.ds(pl.multiple_of(c * W, LANES), W)
        value = conv(raw, ci_ref, at, W).astype(BF16)
        inner[:, at] = value
        weighted = (dot(coef[:T, :], pick[c]) * value.astype(F32)).astype(BF16)
        state[c] = dot(rinT[...], weighted)
        return carry

    lax.fori_loop(0, NC, convolve, 0)

    def onward(c):
        return remote(carry_out.at[c], carry_in.at[c], csend.at[c], crecv.at[c], context=i + 1)

    @pl.when(jnp.logical_not(has_prev))
    def _():
        carry_in[...] = jnp.zeros(carry_in.shape, BF16)

        @pl.when(has_next)
        def _():
            for c in range(NC):
                carry_out[c] = state[c].astype(BF16)
                onward(c).start()

    lane = lax.broadcasted_iota(jnp.int32, (T, LANES), 1)
    per = LANES // PH

    def pair(n):
        at = pl.ds(pl.multiple_of(n * LANES, LANES), LANES)
        cols_of = [
            jnp.sum(jnp.where(lane == n * per + k, run[...], 0.0), axis=1, keepdims=True)
            for k in range(per)
        ]
        for low in (0, B):
            span = slice(low, low + B)
            value = inner[span, at]
            left, right = [], []
            for k in range(per):
                h = n * per + k
                gap = cols_of[k][span, :] - runT[pl.ds(h, 1), :][:, span]
                decay = jnp.exp(jnp.minimum(gap, 0.0))
                left.append((decay * pm[span, span] * stepT[pl.ds(h, 1), :][:, span]).astype(BF16))
                here = (lane[:B, :] >= k * PH) & (lane[:B, :] < (k + 1) * PH)
                right.append(jnp.where(here, value.astype(F32), 0.0).astype(BF16))
            within[span, at] = dot(
                jnp.concatenate(left, axis=1), jnp.concatenate(right, axis=0)
            )

    def chunk(c, squares):
        for n in range(W // LANES):
            pair(c * (W // LANES) + n)
        at = pl.ds(pl.multiple_of(c * W, LANES), W)

        @pl.when(has_prev)
        def _():
            onward(c).wait_recv()

            @pl.when(has_next)
            def _():
                moved = dot(end, pick[c])[:1, :] * carry_in[c].astype(F32) + state[c]
                carry_out[c] = moved.astype(BF16)
                onward(c).start()

        early = (dot(coef[2 * T : 2 * T + B, :], pick[c]) * inner[:B, at].astype(F32)).astype(BF16)
        later = dot(cross, early) * dot(coef[2 * T + B :, :], pick[c])
        within[B:, at] = within[B:, at] + later
        y = within[:, at] + dot(rout[...], carry_in[c]) * dot(coef[T : 2 * T, :], pick[c])
        y = y + skip[c, :1, :] * inner[:, at].astype(F32)
        y = y * gated[:, at]
        gated[:, at] = y
        return squares + jnp.sum(y * y, axis=1, keepdims=True)

    total = lax.fori_loop(0, NC, chunk, jnp.zeros((T, 1), F32))
    sq[...] = jnp.broadcast_to(total, (T, LANES))
    scopies = [
        remote(sq, sq_in.at[n], ssend.at[n], srecv.at[n], tensor=partner)
        for n, partner in enumerate(partners)
    ]
    for copy in scopies:
        copy.start()
    for copy in scopies:
        copy.wait()
    grand = sq[...]
    for n in range(TP - 1):
        grand = grand + sq_in[n]
    factor = wide(lax.rsqrt(grand / (DI * TP) + EPSILON), W)

    def scale_out(c, carry):
        at = pl.ds(pl.multiple_of(c * W, LANES), W)
        inner[:, at] = (gated[:, at] * factor * row_of(og, c)).astype(BF16)
        return carry

    lax.fori_loop(0, NC, scale_out, 0)
    mix_copy = pltpu.make_async_copy(inner, mix_hbm, local_sem.at[9])
    mix_copy.start()

    @pl.when(has_next)
    def _():
        halo.wait_send()
        for c in range(NC):
            onward(c).wait_send()
        for d in range(reach):
            @pl.when(i >= d)
            def _():
                for copy in hop(d):
                    copy.wait_send()

    res_copy.wait()
    mix_copy.wait()


def hand_out(res_in, mix_in, res_out, mix_out, sems):
    copies = []
    for n, (src, dst) in enumerate(((res_in, res_out), (mix_in, mix_out))):
        size = src.shape[0] // PIECES
        for k in range(PIECES):
            at = pl.ds(k * size, size)
            copies.append(pltpu.make_async_copy(src.at[at], dst.at[at], sems.at[n * PIECES + k]))
    for copy in copies:
        copy.start()
    for copy in copies:
        copy.wait()


def per_device(cfg, *args):
    (queries, key_states, value_states, segment_ids, hidden, attn_out_weight, norm_gain,
     gate_weight, inner_weight, state_proj_weight, step_weight, conv_inner, conv_state,
     step_bias, decay_log, skip_gain, out_gain) = args
    T, D = hidden.shape
    DI = inner_weight.shape[1]
    SN = state_proj_weight.shape[1]
    KW = key_states.shape[1]
    TP, C = cfg["tensor"], cfg["context"]
    reach = min(-(-(WINDOW - 1) // T), C - 1)
    cfg = dict(cfg, reach=reach)
    heads = queries.shape[1] // HEAD_DIM
    W = min(512, DI, D)
    NC = DI // W
    hbm = pl.BlockSpec(memory_space=pl.ANY)
    vmem = pl.BlockSpec(memory_space=pltpu.VMEM)
    hops = max(reach, 1)
    peers = max(TP - 1, 1)
    V = pltpu.VMEM
    dma = pltpu.SemaphoreType.DMA
    scratch = [
        V(queries.shape, BF16), V((reach + 1, T, KW), BF16), V((reach + 1, T, KW), BF16),
        V((T, D), BF16), V((TP,) + attn_out_weight.shape, BF16), V(gate_weight.shape, BF16),
        V(inner_weight.shape, BF16), V(state_proj_weight.shape, BF16),
        V((TP,) + queries.shape, BF16),
        V((heads, T, LANES), F32), V((heads, T, LANES), F32), V((heads, T, HEAD_DIM), F32),
        V((T, T), F32), V((T, D), BF16), V((T, D), BF16),
        V((PAD + T, DI), F32), V((PAD + T, SN), F32), V((HALO, DI + SN), BF16),
        V((HALO, DI + SN), BF16), V((PAD + T, LANES), F32), V((CONV - 1, T, LANES), F32),
        V((T, LANES), F32), V((T, LANES), F32), V((LANES, T), F32), V((LANES, T), F32),
        V((T, DI), BF16), V((T, STATE), BF16), V((STATE, T), BF16),
        V((T, STATE), BF16), V((T, T), F32), V((NC, STATE, W), F32), V((NC, STATE, W), BF16),
        V((NC, STATE, W), BF16), V((T, DI), F32), V((T, DI), F32), V((T, LANES), F32),
        V((peers, T, LANES), F32), V((T, D), F32), V((NC, 2 * LANES, W), BF16),
        V((3 * T, 2 * LANES), BF16), V((D // LANES, LANES), F32), V((DI // LANES, LANES), F32),
        V((NC, HALO, W), F32),
        dma((10,)), dma((hops,)), dma((hops,)), dma((hops,)), dma((hops,)),
        dma((peers,)), dma((peers,)), dma((peers,)), dma((peers,)), dma((1,)), dma((1,)),
        dma((NC,)), dma((NC,)), dma((peers,)), dma((peers,)),
    ]
    row = lambda x: x.reshape(1, -1)
    lanes = lambda x: x.reshape(-1, LANES)
    results = pl.pallas_call(
        functools.partial(body, cfg),
        out_shape=(
            jax.ShapeDtypeStruct((T, D), BF16),
            jax.ShapeDtypeStruct((T, DI), BF16),
        ),
        in_specs=[hbm, hbm, hbm, vmem, hbm, hbm, vmem, hbm, hbm, hbm] + [vmem] * 7,
        out_specs=(hbm, hbm),
        scratch_shapes=scratch,
        compiler_params=pltpu.CompilerParams(
            collective_id=0, has_side_effects=True, vmem_limit_bytes=60 * 1024 * 1024
        ),
    )(
        queries, key_states, value_states, row(segment_ids), hidden, attn_out_weight,
        lanes(norm_gain), gate_weight, inner_weight, state_proj_weight, step_weight.T,
        conv_inner, conv_state, row(step_bias), row(decay_log), row(skip_gain), lanes(out_gain),
    )
    return pl.pallas_call(
        hand_out,
        out_shape=tuple(jax.ShapeDtypeStruct(x.shape, x.dtype) for x in results),
        in_specs=[hbm, hbm],
        out_specs=(hbm, hbm),
        scratch_shapes=[dma((2 * PIECES,))],
        compiler_params=pltpu.CompilerParams(vmem_limit_bytes=60 * 1024 * 1024),
    )(*results)


def solution(mesh):
    cfg = {"context": mesh.shape["context"], "tensor": mesh.shape["tensor"]}
    both, tensor = P(("seq", "context"), "tensor"), P("tensor")
    in_specs = (
        both, both, both, P("seq"), P(("seq", "context"), None), P("tensor", None), P(),
        P(None, "tensor"), P(None, "tensor"), P(), P(None, "tensor"), P(None, "tensor"), P(),
        tensor, tensor, tensor, tensor,
    )
    return jax.shard_map(
        functools.partial(per_device, cfg), mesh=mesh, in_specs=in_specs,
        out_specs=(P(("seq", "context"), None), both), check_vma=False,
    )
```

```python
import functools

import jax
import jax.numpy as jnp
from jax import lax
from jax.experimental import pallas as pl
from jax.experimental.pallas import tpu as pltpu
from jax.sharding import PartitionSpec as P

ATT_HEADS = 16
KV_HEADS = 4
HEAD_DIM = 128
STATE = 128
CONV = 4
WINDOW = 2048
EPSILON = 1e-05
LANES = 128
HALO = 16
PAD = 8
PIECES = 4
CHUNK = 512
LOW = -1e30
F32 = jnp.float32
BF16 = jnp.bfloat16


def dot(a, b):
    return jnp.dot(a, b, preferred_element_type=F32)


def silu(x):
    half = 0.5 * x
    return half + half * jnp.tanh(half)


def wide(x, width):
    return jnp.concatenate([x] * (width // LANES), axis=1)


def split(x, parts):
    out = []
    for _ in range(parts):
        piece = x.astype(BF16)
        out.append(piece)
        x = x - piece.astype(F32)
    return out


def body(
    cfg,
    q_hbm, k_hbm, v_hbm, seg_ref, hid_hbm, wo_hbm, gain_ref, wg_hbm, wi_hbm, ws_hbm, wt_ref,
    ci_ref, cs_ref, bias_ref, decay_ref, skip_ref, og_ref,
    res_hbm, mix_hbm,
    q, kbuf, vbuf, hid, wo, wg, wi, ws, att, m_s, l_s, acc, mask, res, normed,
    raw, sraw, halo_out, halo_in, segc, keep, step, run, runT, stepT, inner, rin, rinT, rout,
    pm, state, carry_in, carry_out, within, gated, sq, sq_in, part, pick, coef, gains, og, skip,
    local_sem, ksend, krecv, vsend, vrecv, wsend, wrecv, asend, arecv, hsend, hrecv,
    csend, crecv, ssend, srecv,
):
    C, TP, reach = cfg["context"], cfg["tensor"], cfg["reach"]
    T, D = hid.shape
    DI = wi.shape[1]
    SH = wt_ref.shape[0]
    PH = DI // SH
    heads = q.shape[1] // HEAD_DIM
    groups = ATT_HEADS // KV_HEADS
    NP, _, S = carry_in.shape
    W = min(CHUNK, DI, D)
    NC, cut = DI // W, W // S
    i = lax.axis_index("context")
    core = lax.axis_index("tensor")
    has_next = i + 1 < C
    has_prev = i > 0
    partners = [lax.rem(core + k, TP) for k in range(1, TP)]

    def remote(src, dst, s, r, **where):
        return pltpu.make_async_remote_copy(
            src_ref=src, dst_ref=dst, send_sem=s, recv_sem=r,
            device_id=where, device_id_type=pl.DeviceIdType.MESH,
        )

    barrier = pltpu.get_barrier_semaphore()

    def greet(**where):
        pl.semaphore_signal(
            barrier, inc=1, device_id=where, device_id_type=pl.DeviceIdType.MESH
        )

    @pl.when(has_next)
    def _():
        greet(context=i + 1)

    @pl.when(has_prev)
    def _():
        greet(context=i - 1)

    for partner in partners:
        greet(tensor=partner)

    locals_ = [
        pltpu.make_async_copy(src, dst, local_sem.at[n])
        for n, (src, dst) in enumerate(
            [(q_hbm, q), (k_hbm, kbuf.at[0]), (v_hbm, vbuf.at[0]), (wo_hbm, wo.at[core]),
             (hid_hbm, hid), (ws_hbm, ws), (wi_hbm, wi), (wg_hbm, wg)]
        )
    ]
    for copy in locals_[:3]:
        copy.start()

    pl.semaphore_wait(
        barrier, has_next.astype(jnp.int32) + has_prev.astype(jnp.int32) + TP - 1
    )

    def hop(d):
        to = i + 1
        return (
            remote(kbuf.at[d], kbuf.at[d + 1], ksend.at[d], krecv.at[d], context=to),
            remote(vbuf.at[d], vbuf.at[d + 1], vsend.at[d], vrecv.at[d], context=to),
        )

    locals_[1].wait()
    locals_[2].wait()
    if reach > 0:
        @pl.when(has_next)
        def _():
            for copy in hop(0):
                copy.start()

    for copy in locals_[3:]:
        copy.start()
    wcopies = [
        remote(wo_hbm, wo.at[core], wsend.at[n], wrecv.at[n], tensor=partner)
        for n, partner in enumerate(partners)
    ]
    for copy in wcopies:
        copy.start()

    rows = lax.broadcasted_iota(jnp.int32, (T, T), 0)
    cols = lax.broadcasted_iota(jnp.int32, (T, T), 1)

    def seg_row(block):
        return seg_ref[:, pl.ds(pl.multiple_of(block * T, LANES), T)].astype(F32)

    def column(row):
        return jnp.sum(jnp.where(rows == cols, row, 0.0), axis=1, keepdims=True)

    own_row = seg_row(i)
    own_col = column(own_row)
    prev_col = jnp.where(has_prev, column(seg_row(jnp.maximum(i - 1, 0))), -1.0)
    segc[PAD:, :] = jnp.broadcast_to(own_col, (T, LANES))
    segc[:PAD, :] = jnp.broadcast_to(prev_col[T - PAD :, :], (PAD, LANES))
    for tap in range(CONV - 1):
        keep[tap] = (segc[pl.ds(PAD - CONV + 1 + tap, T), :] == segc[PAD:, :]).astype(F32)

    gains[...] = gain_ref[...].astype(F32)
    og[...] = og_ref[...].astype(F32)

    def row_of(ref, c):
        per = W // LANES
        return jnp.concatenate([ref[pl.ds(c * per + k, 1), :] for k in range(per)], axis=1)

    head_row = lax.broadcasted_iota(jnp.int32, (LANES, W), 0) * PH
    head_col = lax.broadcasted_iota(jnp.int32, (LANES, W), 1)

    def make_pick(c, carry):
        offset = head_col + c * W - head_row
        chosen = jnp.where((offset >= 0) & (offset < PH), 1.0, 0.0).astype(BF16)
        pick[c, :LANES, :] = chosen
        pick[c, LANES:, :] = chosen
        return carry

    lax.fori_loop(0, NC, make_pick, 0)

    def pieces(x):
        return jnp.concatenate(split(x, 2), axis=1)

    gain = jnp.concatenate([skip_ref[...], jnp.zeros((1, LANES - SH), F32)], axis=1)
    gain = pieces(jnp.broadcast_to(gain, (HALO, LANES)))
    for c in range(NC):
        skip[c] = dot(gain, pick[c])

    m_s[...] = jnp.full(m_s.shape, LOW, F32)
    l_s[...] = jnp.zeros(l_s.shape, F32)
    acc[...] = jnp.zeros(acc.shape, F32)
    scale = HEAD_DIM ** (-0.5)

    def attend(d):
        gap = d * T + rows - cols
        key_row = seg_row(i - d)
        allowed = (gap >= 0) & (gap < WINDOW) & (segc[PAD:, :1] == key_row)
        mask[...] = jnp.where(allowed, 0.0, LOW)

        def one(h, carry):
            at = pl.multiple_of(h * HEAD_DIM, HEAD_DIM)
            kat = pl.multiple_of((h // groups) * HEAD_DIM, HEAD_DIM)
            s = lax.dot_general(
                q[:, pl.ds(at, HEAD_DIM)], kbuf[d, :, pl.ds(kat, HEAD_DIM)],
                (((1,), (1,)), ((), ())), preferred_element_type=F32,
            )
            s = s * scale + mask[...]
            old = m_s[h]
            new = jnp.maximum(old, jnp.max(s, axis=1, keepdims=True))
            alpha = jnp.exp(old - new)
            p = jnp.exp(s - wide(new, T))
            m_s[h] = new
            l_s[h] = l_s[h] * alpha + jnp.sum(p, axis=1, keepdims=True)
            acc[h] = acc[h] * alpha + dot(p.astype(BF16), vbuf[d, :, pl.ds(kat, HEAD_DIM)])
            return carry

        lax.fori_loop(0, heads, one, 0, unroll=4)

    locals_[0].wait()
    attend(0)

    if reach > 0:
        def arrive(d, carry):
            @pl.when(i >= d)
            def _():
                for copy in hop(d - 1):
                    copy.wait_recv()

                @pl.when(has_next & (d < reach))
                def _():
                    for copy in hop(d):
                        copy.start()

                attend(d)

            return carry

        lax.fori_loop(1, reach + 1, arrive, 0)

    def finish(h, carry):
        at = pl.multiple_of(h * HEAD_DIM, HEAD_DIM)
        att[core, :, pl.ds(at, HEAD_DIM)] = (acc[h] / l_s[h]).astype(BF16)
        return carry

    lax.fori_loop(0, heads, finish, 0, unroll=2)
    acopies = [
        remote(att.at[core], att.at[core], asend.at[n], arecv.at[n], tensor=partner)
        for n, partner in enumerate(partners)
    ]
    for copy in acopies:
        copy.start()
    locals_[3].wait()

    def project_own(c, carry):
        at = pl.ds(pl.multiple_of(c * W, LANES), W)
        part[:, at] = dot(att[core], wo[core, :, at])
        return carry

    lax.fori_loop(0, D // W, project_own, 0, unroll=2)
    locals_[4].wait()
    for copy in wcopies:
        copy.wait()
    for copy in acopies:
        copy.wait()

    def project(c, squares):
        at = pl.ds(pl.multiple_of(c * W, LANES), W)
        total = part[:, at]
        for partner in partners:
            total = total + dot(att[partner], wo[partner, :, at])
        r = (hid[:, at].astype(F32) + total).astype(BF16)
        res[:, at] = r
        r = r.astype(F32)
        return squares + jnp.sum(r * r, axis=1, keepdims=True)

    squares = lax.fori_loop(0, D // W, project, jnp.zeros((T, 1), F32), unroll=2)
    res_copy = pltpu.make_async_copy(res, res_hbm, local_sem.at[8])
    res_copy.start()
    inv = lax.rsqrt(squares / D + EPSILON)

    def norm(c, carry):
        at = pl.ds(pl.multiple_of(c * W, LANES), W)
        normed[:, at] = (res[:, at].astype(F32) * inv * row_of(gains, c)).astype(BF16)
        return carry

    lax.fori_loop(0, D // W, norm, 0)

    locals_[5].wait()
    x = dot(normed[...], ws[...]).astype(BF16)
    sraw[PAD:, :] = x.astype(F32)
    halo_out[:, DI:] = x[T - HALO :, :]
    locals_[6].wait()

    def project_inner(c, carry):
        at = pl.ds(pl.multiple_of(c * W, LANES), W)
        y = dot(normed[...], wi[:, at]).astype(BF16)
        raw[PAD:, at] = y.astype(F32)
        halo_out[:, at] = y[T - HALO :, :]
        return carry

    lax.fori_loop(0, NC, project_inner, 0, unroll=2)
    halo = remote(halo_out, halo_in, hsend.at[0], hrecv.at[0], context=i + 1)

    @pl.when(has_next)
    def _():
        halo.start()

    raw_step = lax.dot_general(
        normed[...], wt_ref[...], (((1,), (1,)), ((), ())), preferred_element_type=F32
    ) + bias_ref[...]
    soft = jnp.maximum(raw_step, 0.0) + jnp.log1p(jnp.exp(-jnp.abs(raw_step)))
    step[...] = jnp.zeros(step.shape, F32)
    step[:, :SH] = soft
    run[...] = jnp.zeros(run.shape, F32)
    run[:, :SH] = -jnp.exp(decay_ref[...]) * soft
    causal = rows >= cols
    tri = jnp.where(causal, 1.0, 0.0).astype(BF16)
    running = sum(dot(tri, piece) for piece in split(run[...], 3))
    run[...] = running
    runT[...] = running.T
    stepT[...] = step[...].T

    @pl.when(has_prev)
    def _():
        halo.wait_recv()
        raw[:PAD, :] = halo_in[:, :DI].astype(F32)[HALO - PAD :, :]
        sraw[:PAD, :] = halo_in[:, DI:].astype(F32)[HALO - PAD :, :]

    @pl.when(jnp.logical_not(has_prev))
    def _():
        raw[:PAD, :] = jnp.zeros((PAD, DI), F32)
        sraw[:PAD, :] = jnp.zeros((PAD, sraw.shape[1]), F32)

    def conv(ref, taps, at, width):
        total = taps[CONV - 1 : CONV, at].astype(F32) * ref[PAD:, at]
        for tap in range(CONV - 1):
            total = total + (
                taps[tap : tap + 1, at].astype(F32)
                * ref[pl.ds(PAD - CONV + 1 + tap, T), at]
                * wide(keep[tap], width)
            )
        return silu(total)

    sc = conv(sraw, cs_ref, pl.ds(0, 2 * STATE), 2 * STATE)
    rin[...] = sc[:, :STATE].astype(BF16)
    rinT[...] = sc[:, :STATE].T.astype(BF16)
    rout[...] = sc[:, STATE:].astype(BF16)
    pairwise = lax.dot_general(
        rout[...], rin[...], (((1,), (1,)), ((), ())), preferred_element_type=F32
    )
    pm[...] = jnp.where(causal & (segc[PAD:, :1] == own_row), pairwise, 0.0)

    last = run[T - 1 : T, :]
    prior = segc[PAD - 1 : PAD, :]
    tail = jnp.exp(last - run[...]) * step[...]
    tail = jnp.where(segc[PAD:, :] == segc[PAD + T - 1 : PAD + T, :], tail, 0.0)
    B = T // 2
    middle = run[B - 1 : B, :]
    coef[:T, :] = pieces(tail)
    coef[T : 2 * T, :] = pieces(jnp.where(segc[PAD:, :] == prior, jnp.exp(run[...]), 0.0))
    coef[2 * T : 2 * T + B, :] = pieces(jnp.exp(middle - run[:B, :]) * step[:B, :])
    coef[2 * T + B :, :] = pieces(jnp.exp(run[B:, :] - middle))
    end = jnp.where(segc[PAD + T - 1 : PAD + T, :] == prior, jnp.exp(last), 0.0)
    end = pieces(jnp.broadcast_to(end, (HALO, LANES)))
    cross = pm[B:, :B].astype(BF16)

    def onward(p):
        return remote(carry_out.at[p], carry_in.at[p], csend.at[p], crecv.at[p], context=i + 1)

    def convolve(c, carry):
        at = pl.ds(pl.multiple_of(c * W, LANES), W)
        value = conv(raw, ci_ref, at, W).astype(BF16)
        inner[:, at] = value
        weighted = (dot(coef[:T, :], pick[c]) * value.astype(F32)).astype(BF16)
        fresh = dot(rinT[...], weighted)
        for k in range(cut):
            state[c * cut + k] = fresh[:, k * S : (k + 1) * S]

        @pl.when(has_next & jnp.logical_not(has_prev))
        def _():
            for k in range(cut):
                carry_out[c * cut + k] = fresh[:, k * S : (k + 1) * S].astype(BF16)
                onward(c * cut + k).start()

        return carry

    lax.fori_loop(0, NC, convolve, 0)

    @pl.when(jnp.logical_not(has_prev))
    def _():
        carry_in[...] = jnp.zeros(carry_in.shape, BF16)

    locals_[7].wait()
    lane = lax.broadcasted_iota(jnp.int32, (T, LANES), 1)
    per = LANES // PH

    def pair(n):
        at = pl.ds(pl.multiple_of(n * LANES, LANES), LANES)
        cols_of = [
            jnp.sum(jnp.where(lane == n * per + k, run[...], 0.0), axis=1, keepdims=True)
            for k in range(per)
        ]
        for low in (0, B):
            span = slice(low, low + B)
            value = inner[span, at]
            left, right = [], []
            for k in range(per):
                h = n * per + k
                gap = cols_of[k][span, :] - runT[pl.ds(h, 1), :][:, span]
                decay = jnp.exp(jnp.minimum(gap, 0.0))
                left.append((decay * pm[span, span] * stepT[pl.ds(h, 1), :][:, span]).astype(BF16))
                here = (lane[:B, :] >= k * PH) & (lane[:B, :] < (k + 1) * PH)
                right.append(jnp.where(here, value.astype(F32), 0.0).astype(BF16))
            within[span, at] = dot(
                jnp.concatenate(left, axis=1), jnp.concatenate(right, axis=0)
            )

    def chunk(c, squares):
        at = pl.ds(pl.multiple_of(c * W, LANES), W)

        @pl.when(has_prev & has_next)
        def _():
            keeps = dot(end, pick[c])[:1, :]
            for k in range(cut):
                p = c * cut + k
                onward(p).wait_recv()
                moved = keeps[:, k * S : (k + 1) * S] * carry_in[p].astype(F32) + state[p]
                carry_out[p] = moved.astype(BF16)
                onward(p).start()

        gated[:, at] = silu(dot(normed[...], wg[:, at]).astype(BF16).astype(F32))
        for n in range(W // LANES):
            pair(c * (W // LANES) + n)

        @pl.when(has_prev & jnp.logical_not(has_next))
        def _():
            for k in range(cut):
                onward(c * cut + k).wait_recv()

        arrived = jnp.concatenate([carry_in[c * cut + k] for k in range(cut)], axis=1)
        early = (dot(coef[2 * T : 2 * T + B, :], pick[c]) * inner[:B, at].astype(F32)).astype(BF16)
        later = dot(cross, early) * dot(coef[2 * T + B :, :], pick[c])
        within[B:, at] = within[B:, at] + later
        y = within[:, at] + dot(rout[...], arrived) * dot(coef[T : 2 * T, :], pick[c])
        y = y + skip[c, :1, :] * inner[:, at].astype(F32)
        y = y * gated[:, at]
        gated[:, at] = y
        return squares + jnp.sum(y * y, axis=1, keepdims=True)

    total = lax.fori_loop(0, NC, chunk, jnp.zeros((T, 1), F32))
    sq[...] = jnp.broadcast_to(total, (T, LANES))
    scopies = [
        remote(sq, sq_in.at[n], ssend.at[n], srecv.at[n], tensor=partner)
        for n, partner in enumerate(partners)
    ]
    for copy in scopies:
        copy.start()
    for copy in scopies:
        copy.wait()
    grand = sq[...]
    for n in range(TP - 1):
        grand = grand + sq_in[n]
    factor = wide(lax.rsqrt(grand / (DI * TP) + EPSILON), W)

    def scale_out(c, carry):
        at = pl.ds(pl.multiple_of(c * W, LANES), W)
        inner[:, at] = (gated[:, at] * factor * row_of(og, c)).astype(BF16)
        return carry

    lax.fori_loop(0, NC, scale_out, 0)
    mix_copy = pltpu.make_async_copy(inner, mix_hbm, local_sem.at[9])
    mix_copy.start()

    @pl.when(has_next)
    def _():
        halo.wait_send()
        for p in range(NP):
            onward(p).wait_send()
        for d in range(reach):
            @pl.when(i >= d)
            def _():
                for copy in hop(d):
                    copy.wait_send()

    res_copy.wait()
    mix_copy.wait()


def hand_out(res_in, mix_in, res_out, mix_out, res_held, mix_held, sems):
    inward, outward = [], []
    for n, (src, held, dst) in enumerate(
        ((res_in, res_held, res_out), (mix_in, mix_held, mix_out))
    ):
        size = src.shape[0] // PIECES
        for k in range(PIECES):
            at = pl.ds(k * size, size)
            inward.append(
                pltpu.make_async_copy(src.at[at], held.at[at], sems.at[0, n * PIECES + k])
            )
            outward.append(
                pltpu.make_async_copy(held.at[at], dst.at[at], sems.at[1, n * PIECES + k])
            )
    for copy in inward:
        copy.start()
    for first, second in zip(inward, outward):
        first.wait()
        second.start()
    for copy in outward:
        copy.wait()


def per_device(cfg, *args):
    (queries, key_states, value_states, segment_ids, hidden, attn_out_weight, norm_gain,
     gate_weight, inner_weight, state_proj_weight, step_weight, conv_inner, conv_state,
     step_bias, decay_log, skip_gain, out_gain) = args
    T, D = hidden.shape
    DI = inner_weight.shape[1]
    SN = state_proj_weight.shape[1]
    KW = key_states.shape[1]
    TP, C = cfg["tensor"], cfg["context"]
    reach = min(-(-(WINDOW - 1) // T), C - 1)
    cfg = dict(cfg, reach=reach)
    heads = queries.shape[1] // HEAD_DIM
    W = min(CHUNK, DI, D)
    NC = DI // W
    S = min(W, 2 * LANES)
    NP = DI // S
    hbm = pl.BlockSpec(memory_space=pl.ANY)
    vmem = pl.BlockSpec(memory_space=pltpu.VMEM)
    hops = max(reach, 1)
    peers = max(TP - 1, 1)
    V = pltpu.VMEM
    dma = pltpu.SemaphoreType.DMA
    scratch = [
        V(queries.shape, BF16), V((reach + 1, T, KW), BF16), V((reach + 1, T, KW), BF16),
        V((T, D), BF16), V((TP,) + attn_out_weight.shape, BF16), V(gate_weight.shape, BF16),
        V(inner_weight.shape, BF16), V(state_proj_weight.shape, BF16),
        V((TP,) + queries.shape, BF16),
        V((heads, T, LANES), F32), V((heads, T, LANES), F32), V((heads, T, HEAD_DIM), F32),
        V((T, T), F32), V((T, D), BF16), V((T, D), BF16),
        V((PAD + T, DI), F32), V((PAD + T, SN), F32), V((HALO, DI + SN), BF16),
        V((HALO, DI + SN), BF16), V((PAD + T, LANES), F32), V((CONV - 1, T, LANES), F32),
        V((T, LANES), F32), V((T, LANES), F32), V((LANES, T), F32), V((LANES, T), F32),
        V((T, DI), BF16), V((T, STATE), BF16), V((STATE, T), BF16),
        V((T, STATE), BF16), V((T, T), F32), V((NP, STATE, S), F32), V((NP, STATE, S), BF16),
        V((NP, STATE, S), BF16), V((T, DI), F32), V((T, DI), F32), V((T, LANES), F32),
        V((peers, T, LANES), F32), V((T, D), F32), V((NC, 2 * LANES, W), BF16),
        V((3 * T, 2 * LANES), BF16), V((D // LANES, LANES), F32), V((DI // LANES, LANES), F32),
        V((NC, HALO, W), F32),
        dma((10,)), dma((hops,)), dma((hops,)), dma((hops,)), dma((hops,)),
        dma((peers,)), dma((peers,)), dma((peers,)), dma((peers,)), dma((1,)), dma((1,)),
        dma((NP,)), dma((NP,)), dma((peers,)), dma((peers,)),
    ]
    row = lambda x: x.reshape(1, -1)
    lanes = lambda x: x.reshape(-1, LANES)
    results = pl.pallas_call(
        functools.partial(body, cfg),
        out_shape=(
            jax.ShapeDtypeStruct((T, D), BF16),
            jax.ShapeDtypeStruct((T, DI), BF16),
        ),
        in_specs=[hbm, hbm, hbm, vmem, hbm, hbm, vmem, hbm, hbm, hbm] + [vmem] * 7,
        out_specs=(hbm, hbm),
        scratch_shapes=scratch,
        compiler_params=pltpu.CompilerParams(
            collective_id=0, has_side_effects=True, vmem_limit_bytes=60 * 1024 * 1024
        ),
    )(
        queries, key_states, value_states, row(segment_ids), hidden, attn_out_weight,
        lanes(norm_gain), gate_weight, inner_weight, state_proj_weight, step_weight.T,
        conv_inner, conv_state, row(step_bias), row(decay_log), row(skip_gain), lanes(out_gain),
    )
    return pl.pallas_call(
        hand_out,
        out_shape=tuple(jax.ShapeDtypeStruct(x.shape, x.dtype) for x in results),
        in_specs=[hbm, hbm],
        out_specs=(hbm, hbm),
        scratch_shapes=[V((T, D), BF16), V((T, DI), BF16), dma((2, 2 * PIECES))],
        compiler_params=pltpu.CompilerParams(vmem_limit_bytes=60 * 1024 * 1024),
    )(*results)


def solution(mesh):
    cfg = {"context": mesh.shape["context"], "tensor": mesh.shape["tensor"]}
    both, tensor = P(("seq", "context"), "tensor"), P("tensor")
    in_specs = (
        both, both, both, P("seq"), P(("seq", "context"), None), P("tensor", None), P(),
        P(None, "tensor"), P(None, "tensor"), P(), P(None, "tensor"), P(None, "tensor"), P(),
        tensor, tensor, tensor, tensor,
    )
    return jax.shard_map(
        functools.partial(per_device, cfg), mesh=mesh, in_specs=in_specs,
        out_specs=(P(("seq", "context"), None), both), check_vma=False,
    )
```

```python
import functools

import jax
import jax.numpy as jnp
from jax import lax
from jax.experimental import pallas as pl
from jax.experimental.pallas import tpu as pltpu
from jax.sharding import PartitionSpec as P

ATT_HEADS = 16
KV_HEADS = 4
HEAD_DIM = 128
STATE = 128
CONV = 4
WINDOW = 2048
EPSILON = 1e-05
LANES = 128
HALO = 16
PAD = 8
PIECES = 4
CHUNK = 512
LOW = -1e30
F32 = jnp.float32
BF16 = jnp.bfloat16


def dot(a, b):
    return jnp.dot(a, b, preferred_element_type=F32)


def silu(x):
    half = 0.5 * x
    return half + half * jnp.tanh(half)


def wide(x, width):
    return jnp.concatenate([x] * (width // LANES), axis=1)


def split(x, parts):
    out = []
    for _ in range(parts):
        piece = x.astype(BF16)
        out.append(piece)
        x = x - piece.astype(F32)
    return out


def body(
    cfg,
    q_hbm, k_hbm, v_hbm, seg_ref, hid_hbm, wo_hbm, gain_ref, wg_hbm, wi_hbm, ws_hbm, wt_ref,
    ci_ref, cs_ref, bias_ref, decay_ref, skip_ref, og_ref,
    res_hbm, mix_hbm,
    q, kbuf, vbuf, hid, wo, wg, wi, ws, att, m_s, l_s, acc, mask, res, normed,
    raw, sraw, halo_out, halo_in, segc, keep, step, run, runT, stepT, inner, rin, rinT, rout,
    pm, state, carry_in, carry_out, within, gated, sq, sq_in, part, pick, coef, gains, og, skip,
    local_sem, ksend, krecv, vsend, vrecv, wsend, wrecv, asend, arecv, hsend, hrecv,
    csend, crecv, ssend, srecv,
):
    C, TP, reach = cfg["context"], cfg["tensor"], cfg["reach"]
    T, D = hid.shape
    DI = wi.shape[1]
    SH = wt_ref.shape[0]
    PH = DI // SH
    heads = q.shape[1] // HEAD_DIM
    groups = ATT_HEADS // KV_HEADS
    NP, _, S = carry_in.shape
    W = min(CHUNK, DI, D)
    NC, cut = DI // W, W // S
    i = lax.axis_index("context")
    core = lax.axis_index("tensor")
    has_next = i + 1 < C
    has_prev = i > 0
    partners = [lax.rem(core + k, TP) for k in range(1, TP)]

    def remote(src, dst, s, r, **where):
        return pltpu.make_async_remote_copy(
            src_ref=src, dst_ref=dst, send_sem=s, recv_sem=r,
            device_id=where, device_id_type=pl.DeviceIdType.MESH,
        )

    barrier = pltpu.get_barrier_semaphore()

    def greet(**where):
        pl.semaphore_signal(
            barrier, inc=1, device_id=where, device_id_type=pl.DeviceIdType.MESH
        )

    @pl.when(has_next)
    def _():
        greet(context=i + 1)

    @pl.when(has_prev)
    def _():
        greet(context=i - 1)

    for partner in partners:
        greet(tensor=partner)

    locals_ = [
        pltpu.make_async_copy(src, dst, local_sem.at[n])
        for n, (src, dst) in enumerate(
            [(q_hbm, q), (k_hbm, kbuf.at[0]), (v_hbm, vbuf.at[0]), (wo_hbm, wo.at[core]),
             (hid_hbm, hid), (ws_hbm, ws), (wi_hbm, wi), (wg_hbm, wg)]
        )
    ]
    for copy in locals_[:3]:
        copy.start()

    pl.semaphore_wait(
        barrier, has_next.astype(jnp.int32) + has_prev.astype(jnp.int32) + TP - 1
    )

    wcopies = [
        remote(wo_hbm, wo.at[core], wsend.at[n], wrecv.at[n], tensor=partner)
        for n, partner in enumerate(partners)
    ]
    for copy in wcopies:
        copy.start()

    kv_heads = kbuf.shape[2] // HEAD_DIM

    def hop(d, g):
        to = i + 1
        at = pl.ds(g * HEAD_DIM, HEAD_DIM)
        return (
            remote(
                kbuf.at[d, :, at], kbuf.at[d + 1, :, at],
                ksend.at[d, g], krecv.at[d, g], context=to,
            ),
            remote(
                vbuf.at[d, :, at], vbuf.at[d + 1, :, at],
                vsend.at[d, g], vrecv.at[d, g], context=to,
            ),
        )

    locals_[1].wait()
    locals_[2].wait()
    if reach > 0:
        @pl.when(has_next)
        def _():
            for g in range(kv_heads):
                for copy in hop(0, g):
                    copy.start()

    for copy in locals_[3:]:
        copy.start()

    rows = lax.broadcasted_iota(jnp.int32, (T, T), 0)
    cols = lax.broadcasted_iota(jnp.int32, (T, T), 1)

    def seg_row(block):
        return seg_ref[:, pl.ds(pl.multiple_of(block * T, LANES), T)].astype(F32)

    def column(row):
        return jnp.sum(jnp.where(rows == cols, row, 0.0), axis=1, keepdims=True)

    own_row = seg_row(i)
    own_col = column(own_row)
    prev_col = jnp.where(has_prev, column(seg_row(jnp.maximum(i - 1, 0))), -1.0)
    segc[PAD:, :] = jnp.broadcast_to(own_col, (T, LANES))
    segc[:PAD, :] = jnp.broadcast_to(prev_col[T - PAD :, :], (PAD, LANES))
    for tap in range(CONV - 1):
        keep[tap] = (segc[pl.ds(PAD - CONV + 1 + tap, T), :] == segc[PAD:, :]).astype(F32)

    gains[...] = gain_ref[...].astype(F32)
    og[...] = og_ref[...].astype(F32)

    def row_of(ref, c):
        per = W // LANES
        return jnp.concatenate([ref[pl.ds(c * per + k, 1), :] for k in range(per)], axis=1)

    head_row = lax.broadcasted_iota(jnp.int32, (LANES, W), 0) * PH
    head_col = lax.broadcasted_iota(jnp.int32, (LANES, W), 1)

    def make_pick(c, carry):
        offset = head_col + c * W - head_row
        chosen = jnp.where((offset >= 0) & (offset < PH), 1.0, 0.0).astype(BF16)
        pick[c, :LANES, :] = chosen
        pick[c, LANES:, :] = chosen
        return carry

    lax.fori_loop(0, NC, make_pick, 0)

    def pieces(x):
        return jnp.concatenate(split(x, 2), axis=1)

    gain = jnp.concatenate([skip_ref[...], jnp.zeros((1, LANES - SH), F32)], axis=1)
    gain = pieces(jnp.broadcast_to(gain, (HALO, LANES)))
    for c in range(NC):
        skip[c] = dot(gain, pick[c])

    m_s[...] = jnp.full(m_s.shape, LOW, F32)
    l_s[...] = jnp.zeros(l_s.shape, F32)
    acc[...] = jnp.zeros(acc.shape, F32)
    scale = HEAD_DIM ** (-0.5)

    def allow(d):
        gap = d * T + rows - cols
        allowed = (gap >= 0) & (gap < WINDOW) & (segc[PAD:, :1] == seg_row(i - d))
        mask[...] = jnp.where(allowed, 0.0, LOW)

    def attend(d, g):
        kat = pl.ds(g * HEAD_DIM, HEAD_DIM)

        def one(h, carry):
            at = pl.multiple_of(h * HEAD_DIM, HEAD_DIM)
            s = lax.dot_general(
                q[:, pl.ds(at, HEAD_DIM)], kbuf[d, :, kat],
                (((1,), (1,)), ((), ())), preferred_element_type=F32,
            )
            s = s * scale + mask[...]
            old = m_s[h]
            new = jnp.maximum(old, jnp.max(s, axis=1, keepdims=True))
            alpha = jnp.exp(old - new)
            p = jnp.exp(s - wide(new, T))
            m_s[h] = new
            l_s[h] = l_s[h] * alpha + jnp.sum(p, axis=1, keepdims=True)
            acc[h] = acc[h] * alpha + dot(p.astype(BF16), vbuf[d, :, kat])
            return carry

        lax.fori_loop(g * groups, (g + 1) * groups, one, 0, unroll=True)

    locals_[0].wait()
    allow(0)
    for g in range(kv_heads):
        attend(0, g)

    if reach > 0:
        def arrive(d, carry):
            @pl.when(i >= d)
            def _():
                allow(d)
                for g in range(kv_heads):
                    for copy in hop(d - 1, g):
                        copy.wait_recv()

                    @pl.when(has_next & (d < reach))
                    def _():
                        for copy in hop(d, g):
                            copy.start()

                    attend(d, g)

            return carry

        lax.fori_loop(1, reach + 1, arrive, 0)

    def finish(h, carry):
        at = pl.multiple_of(h * HEAD_DIM, HEAD_DIM)
        att[core, :, pl.ds(at, HEAD_DIM)] = (acc[h] / l_s[h]).astype(BF16)
        return carry

    lax.fori_loop(0, heads, finish, 0, unroll=2)
    acopies = [
        remote(att.at[core], att.at[core], asend.at[n], arecv.at[n], tensor=partner)
        for n, partner in enumerate(partners)
    ]
    for copy in acopies:
        copy.start()
    locals_[3].wait()

    def project_own(c, carry):
        at = pl.ds(pl.multiple_of(c * W, LANES), W)
        part[:, at] = dot(att[core], wo[core, :, at])
        return carry

    lax.fori_loop(0, D // W, project_own, 0, unroll=True)
    locals_[4].wait()
    for copy in wcopies:
        copy.wait()
    for copy in acopies:
        copy.wait()

    def project(c, squares):
        at = pl.ds(pl.multiple_of(c * W, LANES), W)
        total = part[:, at]
        for partner in partners:
            total = total + dot(att[partner], wo[partner, :, at])
        r = (hid[:, at].astype(F32) + total).astype(BF16)
        res[:, at] = r
        r = r.astype(F32)
        return squares + jnp.sum(r * r, axis=1, keepdims=True)

    squares = lax.fori_loop(0, D // W, project, jnp.zeros((T, 1), F32), unroll=True)
    res_copy = pltpu.make_async_copy(res, res_hbm, local_sem.at[8])
    res_copy.start()
    locals_[5].wait()
    locals_[6].wait()
    inv = lax.rsqrt(squares / D + EPSILON)

    def norm(c, carry):
        at = pl.ds(pl.multiple_of(c * W, LANES), W)
        normed[:, at] = (res[:, at].astype(F32) * inv * row_of(gains, c)).astype(BF16)
        return carry

    lax.fori_loop(0, D // W, norm, 0, unroll=True)

    x = dot(normed[...], ws[...]).astype(BF16)
    sraw[PAD:, :] = x.astype(F32)
    halo_out[:, DI:] = x[T - HALO :, :]

    def project_inner(c, carry):
        at = pl.ds(pl.multiple_of(c * W, LANES), W)
        y = dot(normed[...], wi[:, at]).astype(BF16)
        raw[PAD:, at] = y.astype(F32)
        halo_out[:, at] = y[T - HALO :, :]
        return carry

    lax.fori_loop(0, NC, project_inner, 0, unroll=True)
    raw_step = lax.dot_general(
        normed[...], wt_ref[...], (((1,), (1,)), ((), ())), preferred_element_type=F32
    ) + bias_ref[...]
    soft = jnp.maximum(raw_step, 0.0) + jnp.log1p(jnp.exp(-jnp.abs(raw_step)))
    step[...] = jnp.zeros(step.shape, F32)
    step[:, :SH] = soft
    run[...] = jnp.zeros(run.shape, F32)
    run[:, :SH] = -jnp.exp(decay_ref[...]) * soft
    causal = rows >= cols
    tri = jnp.where(causal, 1.0, 0.0).astype(BF16)
    running = sum(dot(tri, piece) for piece in split(run[...], 3))
    run[...] = running
    runT[...] = running.T
    stepT[...] = step[...].T
    halo = remote(halo_out, halo_in, hsend.at[0], hrecv.at[0], context=i + 1)

    @pl.when(has_next)
    def _():
        halo.start()

    @pl.when(has_prev)
    def _():
        halo.wait_recv()
        raw[:PAD, :] = halo_in[:, :DI].astype(F32)[HALO - PAD :, :]
        sraw[:PAD, :] = halo_in[:, DI:].astype(F32)[HALO - PAD :, :]

    @pl.when(jnp.logical_not(has_prev))
    def _():
        raw[:PAD, :] = jnp.zeros((PAD, DI), F32)
        sraw[:PAD, :] = jnp.zeros((PAD, sraw.shape[1]), F32)

    def conv(ref, taps, at, width):
        total = taps[CONV - 1 : CONV, at].astype(F32) * ref[PAD:, at]
        for tap in range(CONV - 1):
            total = total + (
                taps[tap : tap + 1, at].astype(F32)
                * ref[pl.ds(PAD - CONV + 1 + tap, T), at]
                * wide(keep[tap], width)
            )
        return silu(total)

    sc = conv(sraw, cs_ref, pl.ds(0, 2 * STATE), 2 * STATE)
    rin[...] = sc[:, :STATE].astype(BF16)
    rinT[...] = sc[:, :STATE].T.astype(BF16)
    rout[...] = sc[:, STATE:].astype(BF16)
    pairwise = lax.dot_general(
        rout[...], rin[...], (((1,), (1,)), ((), ())), preferred_element_type=F32
    )
    pm[...] = jnp.where(causal & (segc[PAD:, :1] == own_row), pairwise, 0.0)

    last = run[T - 1 : T, :]
    prior = segc[PAD - 1 : PAD, :]
    tail = jnp.exp(last - run[...]) * step[...]
    tail = jnp.where(segc[PAD:, :] == segc[PAD + T - 1 : PAD + T, :], tail, 0.0)
    B = T // 2
    middle = run[B - 1 : B, :]
    coef[:T, :] = pieces(tail)
    coef[T : 2 * T, :] = pieces(jnp.where(segc[PAD:, :] == prior, jnp.exp(run[...]), 0.0))
    coef[2 * T : 2 * T + B, :] = pieces(jnp.exp(middle - run[:B, :]) * step[:B, :])
    coef[2 * T + B :, :] = pieces(jnp.exp(run[B:, :] - middle))
    end = jnp.where(segc[PAD + T - 1 : PAD + T, :] == prior, jnp.exp(last), 0.0)
    end = pieces(jnp.broadcast_to(end, (HALO, LANES)))
    cross = pm[B:, :B].astype(BF16)

    def onward(p):
        return remote(carry_out.at[p], carry_in.at[p], csend.at[p], crecv.at[p], context=i + 1)

    def convolve(c, carry):
        at = pl.ds(pl.multiple_of(c * W, LANES), W)
        value = conv(raw, ci_ref, at, W).astype(BF16)
        inner[:, at] = value
        weighted = (dot(coef[:T, :], pick[c]) * value.astype(F32)).astype(BF16)
        fresh = dot(rinT[...], weighted)
        for k in range(cut):
            state[c * cut + k] = fresh[:, k * S : (k + 1) * S]

        @pl.when(has_next & jnp.logical_not(has_prev))
        def _():
            for k in range(cut):
                carry_out[c * cut + k] = fresh[:, k * S : (k + 1) * S].astype(BF16)
                onward(c * cut + k).start()

        return carry

    lax.fori_loop(0, NC, convolve, 0)

    @pl.when(jnp.logical_not(has_prev))
    def _():
        carry_in[...] = jnp.zeros(carry_in.shape, BF16)

    locals_[7].wait()
    lane = lax.broadcasted_iota(jnp.int32, (T, LANES), 1)
    per = LANES // PH

    def pair(n):
        at = pl.ds(pl.multiple_of(n * LANES, LANES), LANES)
        cols_of = [
            jnp.sum(jnp.where(lane == n * per + k, run[...], 0.0), axis=1, keepdims=True)
            for k in range(per)
        ]
        for low in (0, B):
            span = slice(low, low + B)
            value = inner[span, at]
            left, right = [], []
            for k in range(per):
                h = n * per + k
                gap = cols_of[k][span, :] - runT[pl.ds(h, 1), :][:, span]
                decay = jnp.exp(jnp.minimum(gap, 0.0))
                left.append((decay * pm[span, span] * stepT[pl.ds(h, 1), :][:, span]).astype(BF16))
                here = (lane[:B, :] >= k * PH) & (lane[:B, :] < (k + 1) * PH)
                right.append(jnp.where(here, value.astype(F32), 0.0).astype(BF16))
            within[span, at] = dot(
                jnp.concatenate(left, axis=1), jnp.concatenate(right, axis=0)
            )

    def chunk(c, squares):
        at = pl.ds(pl.multiple_of(c * W, LANES), W)

        @pl.when(has_prev & has_next)
        def _():
            keeps = dot(end, pick[c])[:1, :]
            for k in range(cut):
                p = c * cut + k
                onward(p).wait_recv()
                moved = keeps[:, k * S : (k + 1) * S] * carry_in[p].astype(F32) + state[p]
                carry_out[p] = moved.astype(BF16)
                onward(p).start()

        gated[:, at] = silu(dot(normed[...], wg[:, at]).astype(BF16).astype(F32))
        for n in range(W // LANES):
            pair(c * (W // LANES) + n)

        @pl.when(has_prev & jnp.logical_not(has_next))
        def _():
            for k in range(cut):
                onward(c * cut + k).wait_recv()

        arrived = jnp.concatenate([carry_in[c * cut + k] for k in range(cut)], axis=1)
        early = (dot(coef[2 * T : 2 * T + B, :], pick[c]) * inner[:B, at].astype(F32)).astype(BF16)
        later = dot(cross, early) * dot(coef[2 * T + B :, :], pick[c])
        within[B:, at] = within[B:, at] + later
        y = within[:, at] + dot(rout[...], arrived) * dot(coef[T : 2 * T, :], pick[c])
        y = y + skip[c, :1, :] * inner[:, at].astype(F32)
        y = y * gated[:, at]
        gated[:, at] = y
        return squares + jnp.sum(y * y, axis=1, keepdims=True)

    total = lax.fori_loop(0, NC, chunk, jnp.zeros((T, 1), F32))
    sq[...] = jnp.broadcast_to(total, (T, LANES))
    scopies = [
        remote(sq, sq_in.at[n], ssend.at[n], srecv.at[n], tensor=partner)
        for n, partner in enumerate(partners)
    ]
    for copy in scopies:
        copy.start()
    for copy in scopies:
        copy.wait()
    grand = sq[...]
    for n in range(TP - 1):
        grand = grand + sq_in[n]
    factor = wide(lax.rsqrt(grand / (DI * TP) + EPSILON), W)

    def scale_out(c, carry):
        at = pl.ds(pl.multiple_of(c * W, LANES), W)
        inner[:, at] = (gated[:, at] * factor * row_of(og, c)).astype(BF16)
        return carry

    lax.fori_loop(0, NC, scale_out, 0)
    mix_copy = pltpu.make_async_copy(inner, mix_hbm, local_sem.at[9])
    mix_copy.start()

    @pl.when(has_next)
    def _():
        halo.wait_send()
        for p in range(NP):
            onward(p).wait_send()
        for d in range(reach):
            @pl.when(i >= d)
            def _():
                for g in range(kv_heads):
                    for copy in hop(d, g):
                        copy.wait_send()

    res_copy.wait()
    mix_copy.wait()


def hand_out(res_in, mix_in, res_out, mix_out, res_held, mix_held, sems):
    inward, outward = [], []
    for n, (src, held, dst) in enumerate(
        ((res_in, res_held, res_out), (mix_in, mix_held, mix_out))
    ):
        size = src.shape[0] // PIECES
        for k in range(PIECES):
            at = pl.ds(k * size, size)
            inward.append(
                pltpu.make_async_copy(src.at[at], held.at[at], sems.at[0, n * PIECES + k])
            )
            outward.append(
                pltpu.make_async_copy(held.at[at], dst.at[at], sems.at[1, n * PIECES + k])
            )
    for copy in inward:
        copy.start()
    for first, second in zip(inward, outward):
        first.wait()
        second.start()
    for copy in outward:
        copy.wait()


def per_device(cfg, *args):
    (queries, key_states, value_states, segment_ids, hidden, attn_out_weight, norm_gain,
     gate_weight, inner_weight, state_proj_weight, step_weight, conv_inner, conv_state,
     step_bias, decay_log, skip_gain, out_gain) = args
    T, D = hidden.shape
    DI = inner_weight.shape[1]
    SN = state_proj_weight.shape[1]
    KW = key_states.shape[1]
    TP, C = cfg["tensor"], cfg["context"]
    reach = min(-(-(WINDOW - 1) // T), C - 1)
    cfg = dict(cfg, reach=reach)
    heads = queries.shape[1] // HEAD_DIM
    W = min(CHUNK, DI, D)
    NC = DI // W
    S = min(W, 2 * LANES)
    NP = DI // S
    hbm = pl.BlockSpec(memory_space=pl.ANY)
    vmem = pl.BlockSpec(memory_space=pltpu.VMEM)
    hops = max(reach, 1)
    peers = max(TP - 1, 1)
    V = pltpu.VMEM
    dma = pltpu.SemaphoreType.DMA
    scratch = [
        V(queries.shape, BF16), V((reach + 1, T, KW), BF16), V((reach + 1, T, KW), BF16),
        V((T, D), BF16), V((TP,) + attn_out_weight.shape, BF16), V(gate_weight.shape, BF16),
        V(inner_weight.shape, BF16), V(state_proj_weight.shape, BF16),
        V((TP,) + queries.shape, BF16),
        V((heads, T, LANES), F32), V((heads, T, LANES), F32), V((heads, T, HEAD_DIM), F32),
        V((T, T), F32), V((T, D), BF16), V((T, D), BF16),
        V((PAD + T, DI), F32), V((PAD + T, SN), F32), V((HALO, DI + SN), BF16),
        V((HALO, DI + SN), BF16), V((PAD + T, LANES), F32), V((CONV - 1, T, LANES), F32),
        V((T, LANES), F32), V((T, LANES), F32), V((LANES, T), F32), V((LANES, T), F32),
        V((T, DI), BF16), V((T, STATE), BF16), V((STATE, T), BF16),
        V((T, STATE), BF16), V((T, T), F32), V((NP, STATE, S), F32), V((NP, STATE, S), BF16),
        V((NP, STATE, S), BF16), V((T, DI), F32), V((T, DI), F32), V((T, LANES), F32),
        V((peers, T, LANES), F32), V((T, D), F32), V((NC, 2 * LANES, W), BF16),
        V((3 * T, 2 * LANES), BF16), V((D // LANES, LANES), F32), V((DI // LANES, LANES), F32),
        V((NC, HALO, W), F32),
        dma((10,)), dma((hops, KW // HEAD_DIM)), dma((hops, KW // HEAD_DIM)),
        dma((hops, KW // HEAD_DIM)), dma((hops, KW // HEAD_DIM)),
        dma((peers,)), dma((peers,)), dma((peers,)), dma((peers,)), dma((1,)), dma((1,)),
        dma((NP,)), dma((NP,)), dma((peers,)), dma((peers,)),
    ]
    row = lambda x: x.reshape(1, -1)
    lanes = lambda x: x.reshape(-1, LANES)
    results = pl.pallas_call(
        functools.partial(body, cfg),
        out_shape=(
            jax.ShapeDtypeStruct((T, D), BF16),
            jax.ShapeDtypeStruct((T, DI), BF16),
        ),
        in_specs=[hbm, hbm, hbm, vmem, hbm, hbm, vmem, hbm, hbm, hbm] + [vmem] * 7,
        out_specs=(hbm, hbm),
        scratch_shapes=scratch,
        compiler_params=pltpu.CompilerParams(
            collective_id=0, has_side_effects=True, vmem_limit_bytes=60 * 1024 * 1024
        ),
    )(
        queries, key_states, value_states, row(segment_ids), hidden, attn_out_weight,
        lanes(norm_gain), gate_weight, inner_weight, state_proj_weight, step_weight.T,
        conv_inner, conv_state, row(step_bias), row(decay_log), row(skip_gain), lanes(out_gain),
    )
    return pl.pallas_call(
        hand_out,
        out_shape=tuple(jax.ShapeDtypeStruct(x.shape, x.dtype) for x in results),
        in_specs=[hbm, hbm],
        out_specs=(hbm, hbm),
        scratch_shapes=[V((T, D), BF16), V((T, DI), BF16), dma((2, 2 * PIECES))],
        compiler_params=pltpu.CompilerParams(vmem_limit_bytes=60 * 1024 * 1024),
    )(*results)


def solution(mesh):
    cfg = {"context": mesh.shape["context"], "tensor": mesh.shape["tensor"]}
    both, tensor = P(("seq", "context"), "tensor"), P("tensor")
    in_specs = (
        both, both, both, P("seq"), P(("seq", "context"), None), P("tensor", None), P(),
        P(None, "tensor"), P(None, "tensor"), P(), P(None, "tensor"), P(None, "tensor"), P(),
        tensor, tensor, tensor, tensor,
    )
    return jax.shard_map(
        functools.partial(per_device, cfg), mesh=mesh, in_specs=in_specs,
        out_specs=(P(("seq", "context"), None), both), check_vma=False,
    )
```

```python
import functools

import jax
import jax.numpy as jnp
from jax import lax
from jax.experimental import pallas as pl
from jax.experimental.pallas import tpu as pltpu
from jax.sharding import PartitionSpec as P

ATT_HEADS = 16
KV_HEADS = 4
HEAD_DIM = 128
STATE = 128
CONV = 4
WINDOW = 2048
EPSILON = 1e-05
LANES = 128
HALO = 16
PAD = 8
PIECES = 4
CHUNK = 512
LOW = -1e30
F32 = jnp.float32
BF16 = jnp.bfloat16


def dot(a, b):
    return jnp.dot(a, b, preferred_element_type=F32)


def silu(x):
    half = 0.5 * x
    return half + half * jnp.tanh(half)


def wide(x, width):
    return jnp.concatenate([x] * (width // LANES), axis=1)


def split(x, parts):
    out = []
    for _ in range(parts):
        piece = x.astype(BF16)
        out.append(piece)
        x = x - piece.astype(F32)
    return out


def body(
    cfg,
    q_hbm, k_hbm, v_hbm, seg_hbm, hid_hbm, wo_hbm, gain_hbm, wg_hbm, wi_hbm, ws_hbm, wt_hbm,
    ci_hbm, cs_hbm, bias_hbm, decay_hbm, skip_hbm, og_hbm,
    res_hbm, mix_hbm,
    q, kbuf, vbuf, hid, wo, wg, wi, ws, att, m_s, l_s, acc, mask, res, normed,
    raw, sraw, halo_out, halo_in, segc, keep, step, run, runT, stepT, inner, rin, rinT, rout,
    pm, state, carry_in, carry_out, within, gated, sq, sq_in, part, pick, coef, gains, og, skip,
    local_sem, ksend, krecv, vsend, vrecv, wsend, wrecv, asend, arecv, hsend, hrecv,
    csend, crecv, ssend, srecv,
    seg_ref, gain_ref, wt_ref, ci_ref, cs_ref, bias_ref, decay_ref, skip_ref, og_ref, small_sem,
):
    C, TP, reach = cfg["context"], cfg["tensor"], cfg["reach"]
    T, D = hid.shape
    DI = wi.shape[1]
    SH = wt_ref.shape[0]
    PH = DI // SH
    heads = q.shape[1] // HEAD_DIM
    groups = ATT_HEADS // KV_HEADS
    NP, _, S = carry_in.shape
    W = min(CHUNK, DI, D)
    NC, cut = DI // W, W // S
    i = lax.axis_index("context")
    core = lax.axis_index("tensor")
    has_next = i + 1 < C
    has_prev = i > 0
    partners = [lax.rem(core + k, TP) for k in range(1, TP)]

    def remote(src, dst, s, r, **where):
        return pltpu.make_async_remote_copy(
            src_ref=src, dst_ref=dst, send_sem=s, recv_sem=r,
            device_id=where, device_id_type=pl.DeviceIdType.MESH,
        )

    barrier = pltpu.get_barrier_semaphore()

    def greet(**where):
        pl.semaphore_signal(
            barrier, inc=1, device_id=where, device_id_type=pl.DeviceIdType.MESH
        )

    @pl.when(has_next)
    def _():
        greet(context=i + 1)

    @pl.when(has_prev)
    def _():
        greet(context=i - 1)

    for partner in partners:
        greet(tensor=partner)

    locals_ = [
        pltpu.make_async_copy(src, dst, local_sem.at[n])
        for n, (src, dst) in enumerate(
            [(q_hbm, q), (k_hbm, kbuf.at[0]), (v_hbm, vbuf.at[0]), (wo_hbm, wo.at[core]),
             (hid_hbm, hid), (ws_hbm, ws), (wi_hbm, wi), (wg_hbm, wg)]
        )
    ]
    small = [
        pltpu.make_async_copy(src, dst, small_sem.at[n])
        for n, (src, dst) in enumerate(
            [(seg_hbm, seg_ref), (gain_hbm, gain_ref), (og_hbm, og_ref), (skip_hbm, skip_ref),
             (wt_hbm, wt_ref), (ci_hbm, ci_ref), (cs_hbm, cs_ref), (bias_hbm, bias_ref),
             (decay_hbm, decay_ref)]
        )
    ]

    pl.semaphore_wait(
        barrier, has_next.astype(jnp.int32) + has_prev.astype(jnp.int32) + TP - 1
    )

    wcopies = [
        remote(wo_hbm, wo.at[core], wsend.at[n], wrecv.at[n], tensor=partner)
        for n, partner in enumerate(partners)
    ]
    kv_heads = kbuf.shape[2] // HEAD_DIM

    def hop(d, g):
        to = i + 1
        at = pl.ds(g * HEAD_DIM, HEAD_DIM)
        first = isinstance(d, int) and d == 0
        return (
            remote(
                k_hbm.at[:, at] if first else kbuf.at[d, :, at], kbuf.at[d + 1, :, at],
                ksend.at[d, g], krecv.at[d, g], context=to,
            ),
            remote(
                v_hbm.at[:, at] if first else vbuf.at[d, :, at], vbuf.at[d + 1, :, at],
                vsend.at[d, g], vrecv.at[d, g], context=to,
            ),
        )

    if reach > 0:
        @pl.when(has_next)
        def _():
            for g in range(kv_heads):
                for copy in hop(0, g):
                    copy.start()

    for copy in small[:4] + locals_[:3] + wcopies + locals_[3:] + small[4:]:
        copy.start()
    for copy in small[:4]:
        copy.wait()

    rows = lax.broadcasted_iota(jnp.int32, (T, T), 0)
    cols = lax.broadcasted_iota(jnp.int32, (T, T), 1)

    def seg_row(block):
        return seg_ref[:, pl.ds(pl.multiple_of(block * T, LANES), T)].astype(F32)

    def column(row):
        return jnp.sum(jnp.where(rows == cols, row, 0.0), axis=1, keepdims=True)

    own_row = seg_row(i)
    own_col = column(own_row)
    prev_col = jnp.where(has_prev, column(seg_row(jnp.maximum(i - 1, 0))), -1.0)
    segc[PAD:, :] = jnp.broadcast_to(own_col, (T, LANES))
    segc[:PAD, :] = jnp.broadcast_to(prev_col[T - PAD :, :], (PAD, LANES))
    for tap in range(CONV - 1):
        keep[tap] = (segc[pl.ds(PAD - CONV + 1 + tap, T), :] == segc[PAD:, :]).astype(F32)

    gains[...] = gain_ref[...].astype(F32)
    og[...] = og_ref[...].astype(F32)

    def row_of(ref, c):
        per = W // LANES
        return jnp.concatenate([ref[pl.ds(c * per + k, 1), :] for k in range(per)], axis=1)

    head_row = lax.broadcasted_iota(jnp.int32, (LANES, W), 0) * PH
    head_col = lax.broadcasted_iota(jnp.int32, (LANES, W), 1)

    def make_pick(c, carry):
        offset = head_col + c * W - head_row
        chosen = jnp.where((offset >= 0) & (offset < PH), 1.0, 0.0).astype(BF16)
        pick[c, :LANES, :] = chosen
        pick[c, LANES:, :] = chosen
        return carry

    lax.fori_loop(0, NC, make_pick, 0)

    def pieces(x):
        return jnp.concatenate(split(x, 2), axis=1)

    gain = jnp.concatenate([skip_ref[...], jnp.zeros((1, LANES - SH), F32)], axis=1)
    gain = pieces(jnp.broadcast_to(gain, (HALO, LANES)))
    for c in range(NC):
        skip[c] = dot(gain, pick[c])

    m_s[...] = jnp.full(m_s.shape, LOW, F32)
    l_s[...] = jnp.zeros(l_s.shape, F32)
    acc[...] = jnp.zeros(acc.shape, F32)
    scale = HEAD_DIM ** (-0.5)

    def allow(d):
        gap = d * T + rows - cols
        allowed = (gap >= 0) & (gap < WINDOW) & (segc[PAD:, :1] == seg_row(i - d))
        mask[...] = jnp.where(allowed, 0.0, LOW)

    def attend(d, g):
        kat = pl.ds(g * HEAD_DIM, HEAD_DIM)

        def one(h, carry):
            at = pl.multiple_of(h * HEAD_DIM, HEAD_DIM)
            s = lax.dot_general(
                q[:, pl.ds(at, HEAD_DIM)], kbuf[d, :, kat],
                (((1,), (1,)), ((), ())), preferred_element_type=F32,
            )
            s = s * scale + mask[...]
            old = m_s[h]
            new = jnp.maximum(old, jnp.max(s, axis=1, keepdims=True))
            alpha = jnp.exp(old - new)
            p = jnp.exp(s - wide(new, T))
            m_s[h] = new
            l_s[h] = l_s[h] * alpha + jnp.sum(p, axis=1, keepdims=True)
            acc[h] = acc[h] * alpha + dot(p.astype(BF16), vbuf[d, :, kat])
            return carry

        lax.fori_loop(g * groups, (g + 1) * groups, one, 0, unroll=True)

    for copy in locals_[:3]:
        copy.wait()
    allow(0)
    for g in range(kv_heads):
        attend(0, g)

    if reach > 0:
        def arrive(d, carry):
            @pl.when(i >= d)
            def _():
                allow(d)
                for g in range(kv_heads):
                    for copy in hop(d - 1, g):
                        copy.wait_recv()

                    @pl.when(has_next & (d < reach))
                    def _():
                        for copy in hop(d, g):
                            copy.start()

                    attend(d, g)

            return carry

        lax.fori_loop(1, reach + 1, arrive, 0)

    def finish(h, carry):
        at = pl.multiple_of(h * HEAD_DIM, HEAD_DIM)
        att[core, :, pl.ds(at, HEAD_DIM)] = (acc[h] / l_s[h]).astype(BF16)
        return carry

    lax.fori_loop(0, heads, finish, 0, unroll=2)
    acopies = [
        remote(att.at[core], att.at[core], asend.at[n], arecv.at[n], tensor=partner)
        for n, partner in enumerate(partners)
    ]
    for copy in acopies:
        copy.start()
    locals_[3].wait()

    def project_own(c, carry):
        at = pl.ds(pl.multiple_of(c * W, LANES), W)
        part[:, at] = dot(att[core], wo[core, :, at])
        return carry

    lax.fori_loop(0, D // W, project_own, 0, unroll=True)
    locals_[4].wait()
    for copy in wcopies:
        copy.wait()
    for copy in acopies:
        copy.wait()

    def project(c, squares):
        at = pl.ds(pl.multiple_of(c * W, LANES), W)
        total = part[:, at]
        for partner in partners:
            total = total + dot(att[partner], wo[partner, :, at])
        r = (hid[:, at].astype(F32) + total).astype(BF16)
        res[:, at] = r
        r = r.astype(F32)
        return squares + jnp.sum(r * r, axis=1, keepdims=True)

    squares = lax.fori_loop(0, D // W, project, jnp.zeros((T, 1), F32), unroll=True)
    res_copy = pltpu.make_async_copy(res, res_hbm, local_sem.at[8])
    res_copy.start()
    locals_[5].wait()
    locals_[6].wait()
    for copy in small[4:]:
        copy.wait()
    inv = lax.rsqrt(squares / D + EPSILON)

    def norm(c, carry):
        at = pl.ds(pl.multiple_of(c * W, LANES), W)
        normed[:, at] = (res[:, at].astype(F32) * inv * row_of(gains, c)).astype(BF16)
        return carry

    lax.fori_loop(0, D // W, norm, 0, unroll=True)

    x = dot(normed[...], ws[...]).astype(BF16)
    sraw[PAD:, :] = x.astype(F32)
    halo_out[:, DI:] = x[T - HALO :, :]

    def project_inner(c, carry):
        at = pl.ds(pl.multiple_of(c * W, LANES), W)
        y = dot(normed[...], wi[:, at]).astype(BF16)
        raw[PAD:, at] = y.astype(F32)
        halo_out[:, at] = y[T - HALO :, :]
        return carry

    lax.fori_loop(0, NC, project_inner, 0, unroll=True)
    raw_step = lax.dot_general(
        normed[...], wt_ref[...], (((1,), (1,)), ((), ())), preferred_element_type=F32
    ) + bias_ref[...]
    soft = jnp.maximum(raw_step, 0.0) + jnp.log1p(jnp.exp(-jnp.abs(raw_step)))
    step[...] = jnp.zeros(step.shape, F32)
    step[:, :SH] = soft
    run[...] = jnp.zeros(run.shape, F32)
    run[:, :SH] = -jnp.exp(decay_ref[...]) * soft
    causal = rows >= cols
    tri = jnp.where(causal, 1.0, 0.0).astype(BF16)
    running = sum(dot(tri, piece) for piece in split(run[...], 3))
    run[...] = running
    runT[...] = running.T
    stepT[...] = step[...].T
    halo = remote(halo_out, halo_in, hsend.at[0], hrecv.at[0], context=i + 1)

    @pl.when(has_next)
    def _():
        halo.start()

    @pl.when(has_prev)
    def _():
        halo.wait_recv()
        raw[:PAD, :] = halo_in[:, :DI].astype(F32)[HALO - PAD :, :]
        sraw[:PAD, :] = halo_in[:, DI:].astype(F32)[HALO - PAD :, :]

    @pl.when(jnp.logical_not(has_prev))
    def _():
        raw[:PAD, :] = jnp.zeros((PAD, DI), F32)
        sraw[:PAD, :] = jnp.zeros((PAD, sraw.shape[1]), F32)

    def conv(ref, taps, at, width):
        total = taps[CONV - 1 : CONV, at].astype(F32) * ref[PAD:, at]
        for tap in range(CONV - 1):
            total = total + (
                taps[tap : tap + 1, at].astype(F32)
                * ref[pl.ds(PAD - CONV + 1 + tap, T), at]
                * wide(keep[tap], width)
            )
        return silu(total)

    sc = conv(sraw, cs_ref, pl.ds(0, 2 * STATE), 2 * STATE)
    rin[...] = sc[:, :STATE].astype(BF16)
    rinT[...] = sc[:, :STATE].T.astype(BF16)
    rout[...] = sc[:, STATE:].astype(BF16)
    pairwise = lax.dot_general(
        rout[...], rin[...], (((1,), (1,)), ((), ())), preferred_element_type=F32
    )
    pm[...] = jnp.where(causal & (segc[PAD:, :1] == own_row), pairwise, 0.0)

    last = run[T - 1 : T, :]
    prior = segc[PAD - 1 : PAD, :]
    tail = jnp.exp(last - run[...]) * step[...]
    tail = jnp.where(segc[PAD:, :] == segc[PAD + T - 1 : PAD + T, :], tail, 0.0)
    B = T // 2
    middle = run[B - 1 : B, :]
    coef[:T, :] = pieces(tail)
    coef[T : 2 * T, :] = pieces(jnp.where(segc[PAD:, :] == prior, jnp.exp(run[...]), 0.0))
    coef[2 * T : 2 * T + B, :] = pieces(jnp.exp(middle - run[:B, :]) * step[:B, :])
    coef[2 * T + B :, :] = pieces(jnp.exp(run[B:, :] - middle))
    end = jnp.where(segc[PAD + T - 1 : PAD + T, :] == prior, jnp.exp(last), 0.0)
    end = pieces(jnp.broadcast_to(end, (HALO, LANES)))
    cross = pm[B:, :B].astype(BF16)

    def onward(p):
        return remote(carry_out.at[p], carry_in.at[p], csend.at[p], crecv.at[p], context=i + 1)

    def convolve(c, carry):
        at = pl.ds(pl.multiple_of(c * W, LANES), W)
        value = conv(raw, ci_ref, at, W).astype(BF16)
        inner[:, at] = value
        weighted = (dot(coef[:T, :], pick[c]) * value.astype(F32)).astype(BF16)
        fresh = dot(rinT[...], weighted)
        for k in range(cut):
            state[c * cut + k] = fresh[:, k * S : (k + 1) * S]

        @pl.when(has_next & jnp.logical_not(has_prev))
        def _():
            for k in range(cut):
                carry_out[c * cut + k] = fresh[:, k * S : (k + 1) * S].astype(BF16)
                onward(c * cut + k).start()

        return carry

    lax.fori_loop(0, NC, convolve, 0)

    @pl.when(jnp.logical_not(has_prev))
    def _():
        carry_in[...] = jnp.zeros(carry_in.shape, BF16)

    locals_[7].wait()
    lane = lax.broadcasted_iota(jnp.int32, (T, LANES), 1)
    per = LANES // PH

    def pair(n):
        at = pl.ds(pl.multiple_of(n * LANES, LANES), LANES)
        cols_of = [
            jnp.sum(jnp.where(lane == n * per + k, run[...], 0.0), axis=1, keepdims=True)
            for k in range(per)
        ]
        for low in (0, B):
            span = slice(low, low + B)
            value = inner[span, at]
            left, right = [], []
            for k in range(per):
                h = n * per + k
                gap = cols_of[k][span, :] - runT[pl.ds(h, 1), :][:, span]
                decay = jnp.exp(jnp.minimum(gap, 0.0))
                left.append((decay * pm[span, span] * stepT[pl.ds(h, 1), :][:, span]).astype(BF16))
                here = (lane[:B, :] >= k * PH) & (lane[:B, :] < (k + 1) * PH)
                right.append(jnp.where(here, value.astype(F32), 0.0).astype(BF16))
            within[span, at] = dot(
                jnp.concatenate(left, axis=1), jnp.concatenate(right, axis=0)
            )

    def chunk(c, squares):
        at = pl.ds(pl.multiple_of(c * W, LANES), W)

        @pl.when(has_prev & has_next)
        def _():
            keeps = dot(end, pick[c])[:1, :]
            for k in range(cut):
                p = c * cut + k
                onward(p).wait_recv()
                moved = keeps[:, k * S : (k + 1) * S] * carry_in[p].astype(F32) + state[p]
                carry_out[p] = moved.astype(BF16)
                onward(p).start()

        gated[:, at] = silu(dot(normed[...], wg[:, at]).astype(BF16).astype(F32))
        for n in range(W // LANES):
            pair(c * (W // LANES) + n)

        @pl.when(has_prev & jnp.logical_not(has_next))
        def _():
            for k in range(cut):
                onward(c * cut + k).wait_recv()

        arrived = jnp.concatenate([carry_in[c * cut + k] for k in range(cut)], axis=1)
        early = (dot(coef[2 * T : 2 * T + B, :], pick[c]) * inner[:B, at].astype(F32)).astype(BF16)
        later = dot(cross, early) * dot(coef[2 * T + B :, :], pick[c])
        within[B:, at] = within[B:, at] + later
        y = within[:, at] + dot(rout[...], arrived) * dot(coef[T : 2 * T, :], pick[c])
        y = y + skip[c, :1, :] * inner[:, at].astype(F32)
        y = y * gated[:, at]
        gated[:, at] = y
        return squares + jnp.sum(y * y, axis=1, keepdims=True)

    total = lax.fori_loop(0, NC, chunk, jnp.zeros((T, 1), F32))
    sq[...] = jnp.broadcast_to(total, (T, LANES))
    scopies = [
        remote(sq, sq_in.at[n], ssend.at[n], srecv.at[n], tensor=partner)
        for n, partner in enumerate(partners)
    ]
    for copy in scopies:
        copy.start()
    for copy in scopies:
        copy.wait()
    grand = sq[...]
    for n in range(TP - 1):
        grand = grand + sq_in[n]
    factor = wide(lax.rsqrt(grand / (DI * TP) + EPSILON), W)

    mix_copies = []
    for c in range(NC):
        at = pl.ds(c * W, W)
        inner[:, at] = (gated[:, at] * factor * row_of(og, c)).astype(BF16)
        mix_copies.append(
            pltpu.make_async_copy(inner.at[:, at], mix_hbm.at[:, at], local_sem.at[9 + c])
        )
        mix_copies[-1].start()

    @pl.when(has_next)
    def _():
        halo.wait_send()
        for p in range(NP):
            onward(p).wait_send()
        for d in range(reach):
            @pl.when(i >= d)
            def _():
                for g in range(kv_heads):
                    for copy in hop(d, g):
                        copy.wait_send()

    res_copy.wait()
    for copy in mix_copies:
        copy.wait()


def hand_out(res_in, mix_in, res_out, mix_out, res_held, mix_held, sems):
    inward, outward = [], []
    for n, (src, held, dst) in enumerate(
        ((res_in, res_held, res_out), (mix_in, mix_held, mix_out))
    ):
        size = src.shape[0] // PIECES
        for k in range(PIECES):
            at = pl.ds(k * size, size)
            inward.append(
                pltpu.make_async_copy(src.at[at], held.at[at], sems.at[0, n * PIECES + k])
            )
            outward.append(
                pltpu.make_async_copy(held.at[at], dst.at[at], sems.at[1, n * PIECES + k])
            )
    for copy in inward:
        copy.start()
    for first, second in zip(inward, outward):
        first.wait()
        second.start()
    for copy in outward:
        copy.wait()


def per_device(cfg, *args):
    (queries, key_states, value_states, segment_ids, hidden, attn_out_weight, norm_gain,
     gate_weight, inner_weight, state_proj_weight, step_weight, conv_inner, conv_state,
     step_bias, decay_log, skip_gain, out_gain) = args
    T, D = hidden.shape
    DI = inner_weight.shape[1]
    SN = state_proj_weight.shape[1]
    KW = key_states.shape[1]
    TP, C = cfg["tensor"], cfg["context"]
    reach = min(-(-(WINDOW - 1) // T), C - 1)
    cfg = dict(cfg, reach=reach)
    heads = queries.shape[1] // HEAD_DIM
    W = min(CHUNK, DI, D)
    NC = DI // W
    S = min(W, 2 * LANES)
    NP = DI // S
    hbm = pl.BlockSpec(memory_space=pl.ANY)
    hops = max(reach, 1)
    peers = max(TP - 1, 1)
    V = pltpu.VMEM
    dma = pltpu.SemaphoreType.DMA
    scratch = [
        V(queries.shape, BF16), V((reach + 1, T, KW), BF16), V((reach + 1, T, KW), BF16),
        V((T, D), BF16), V((TP,) + attn_out_weight.shape, BF16), V(gate_weight.shape, BF16),
        V(inner_weight.shape, BF16), V(state_proj_weight.shape, BF16),
        V((TP,) + queries.shape, BF16),
        V((heads, T, LANES), F32), V((heads, T, LANES), F32), V((heads, T, HEAD_DIM), F32),
        V((T, T), F32), V((T, D), BF16), V((T, D), BF16),
        V((PAD + T, DI), F32), V((PAD + T, SN), F32), V((HALO, DI + SN), BF16),
        V((HALO, DI + SN), BF16), V((PAD + T, LANES), F32), V((CONV - 1, T, LANES), F32),
        V((T, LANES), F32), V((T, LANES), F32), V((LANES, T), F32), V((LANES, T), F32),
        V((T, DI), BF16), V((T, STATE), BF16), V((STATE, T), BF16),
        V((T, STATE), BF16), V((T, T), F32), V((NP, STATE, S), F32), V((NP, STATE, S), BF16),
        V((NP, STATE, S), BF16), V((T, DI), F32), V((T, DI), F32), V((T, LANES), F32),
        V((peers, T, LANES), F32), V((T, D), F32), V((NC, 2 * LANES, W), BF16),
        V((3 * T, 2 * LANES), BF16), V((D // LANES, LANES), F32), V((DI // LANES, LANES), F32),
        V((NC, HALO, W), F32),
        dma((9 + NC,)), dma((hops, KW // HEAD_DIM)), dma((hops, KW // HEAD_DIM)),
        dma((hops, KW // HEAD_DIM)), dma((hops, KW // HEAD_DIM)),
        dma((peers,)), dma((peers,)), dma((peers,)), dma((peers,)), dma((1,)), dma((1,)),
        dma((NP,)), dma((NP,)), dma((peers,)), dma((peers,)),
    ]
    row = lambda x: x.reshape(1, -1)
    lanes = lambda x: x.reshape(-1, LANES)
    small = [
        row(segment_ids), lanes(norm_gain), step_weight.T, conv_inner, conv_state,
        row(step_bias), row(decay_log), row(skip_gain), lanes(out_gain),
    ]
    scratch += [V(x.shape, x.dtype) for x in small] + [dma((len(small),))]
    results = pl.pallas_call(
        functools.partial(body, cfg),
        out_shape=(
            jax.ShapeDtypeStruct((T, D), BF16),
            jax.ShapeDtypeStruct((T, DI), BF16),
        ),
        in_specs=[hbm] * 17,
        out_specs=(hbm, hbm),
        scratch_shapes=scratch,
        compiler_params=pltpu.CompilerParams(
            collective_id=0, has_side_effects=True, vmem_limit_bytes=60 * 1024 * 1024
        ),
    )(
        queries, key_states, value_states, row(segment_ids), hidden, attn_out_weight,
        lanes(norm_gain), gate_weight, inner_weight, state_proj_weight, step_weight.T,
        conv_inner, conv_state, row(step_bias), row(decay_log), row(skip_gain), lanes(out_gain),
    )
    return pl.pallas_call(
        hand_out,
        out_shape=tuple(jax.ShapeDtypeStruct(x.shape, x.dtype) for x in results),
        in_specs=[hbm, hbm],
        out_specs=(hbm, hbm),
        scratch_shapes=[V((T, D), BF16), V((T, DI), BF16), dma((2, 2 * PIECES))],
        compiler_params=pltpu.CompilerParams(vmem_limit_bytes=60 * 1024 * 1024),
    )(*results)


def solution(mesh):
    cfg = {"context": mesh.shape["context"], "tensor": mesh.shape["tensor"]}
    both, tensor = P(("seq", "context"), "tensor"), P("tensor")
    in_specs = (
        both, both, both, P("seq"), P(("seq", "context"), None), P("tensor", None), P(),
        P(None, "tensor"), P(None, "tensor"), P(), P(None, "tensor"), P(None, "tensor"), P(),
        tensor, tensor, tensor, tensor,
    )
    return jax.shard_map(
        functools.partial(per_device, cfg), mesh=mesh, in_specs=in_specs,
        out_specs=(P(("seq", "context"), None), both), check_vma=False,
    )
```
